128 devices in a mesh: arc: 8 (over y, x_hi), trow: 4 (over z), tcol: 4 (over x_lo, core).
Axes of the slice: x: 4 (x_hi: 2, x_lo: 2; x = x_hi * 2 + x_lo), y: 4, z: 4, core: 2. Of those that a mesh axis runs over, the one named last changes fastest.
Arguments:
- design: bfloat16 [5120, 8192], P('arc', 'tcol'), may hold values from -0.125 to 0.125
- local_design: bfloat16 [5120, 128], P('arc'), may hold values from -0.3125 to 0.3125
- lengths: int32 [16], P('arc'), may hold values from 1 to 320, 3840 in all
- regularizer: float32 [8192], P(('arc', 'trow')), may hold values from 0.2 to 2
Outputs:
- normal: float32 [8192, 8192], P(('arc', 'trow'), 'tcol')
- panel_factor: float32 [2, 8192, 512], P(None, 'tcol')
The draws below stay inside these ranges and needn't reach their ends.
Inputs may be any that keep to these rules, and one draw needn't show every extreme that they name: `lengths`: each arc has at least one live row; some arc is full.
All inputs are finite; a program needn't handle non-finite values. No bound on the sum of `lengths` on one device may be relied on, other than what follows from the above.
Results may differ from the reference program's by a relative error of at most 0.003.
Values may be sent and summed in bfloat16 or wider, within the bound.
A program may use at most 128 MiB of HBM per device.

```python
import math
import jax
import jax.numpy as jnp
import numpy as np
from jax import lax

G = 8192
LOCAL = 128
PANEL = 512
PANELS = 2
CAP = 320
ARCS = 16
ROWS = 5120


def strengthened(result, rng, source, target, blocks, factor):
    def block_of(position):
        return (jnp.arange(result.shape[position]) // (result.shape[position] // blocks)).reshape((-1,) + (1,) * (result.ndim - 1 - position))

    one_side = jax.random.permutation(rng, blocks)[block_of(target)]
    second = (block_of(target) + blocks // 2) % blocks
    return jnp.where((block_of(source) == one_side) | (block_of(source) == second), factor * result, result)


def block_scale(key, extent, split, smallest, largest):
    level, own = 1.0, jax.random.fold_in(key, 6)
    for position, blocks in split:
        steps = jnp.exp(jax.random.uniform(jax.random.fold_in(own, position), (blocks,), jnp.float32, smallest / len(split), largest / len(split)))
        level = level * jnp.repeat(steps, extent[position] // blocks).reshape([-1 if axis == position else 1 for axis in range(len(extent))])
    return level


def profile(amount, total, bound, lean):
    loads = [(1 << 20) // math.isqrt(standing ** lean) + 1 for standing in range(2, amount + 1)]
    surplus, given = total - bound - (amount - 1), [1] * (amount - 1)
    while surplus > 0:
        free = [i for i in range(amount - 1) if given[i] < bound]
        pool, remaining = sum([loads[i] for i in free]), surplus
        for i in free:
            extra = min(bound - given[i], max(1, remaining * loads[i] // pool), surplus)
            given[i] = given[i] + extra
            surplus = surplus - extra
    return np.array([bound] + given)


def uneven_parts(rng, amount, total, reach, slope):
    if amount == 2:
        one = jax.random.randint(rng, (), max(1, total - reach), min(reach, total - 1) + 1)
        return jnp.stack([one, total - one])
    sizes = jnp.asarray(profile(amount, total, reach, slope), jnp.int32)
    pairs = (amount - 1) // 2
    source_of, sink = sizes[1:1 + 2 * pairs:2], sizes[2:2 + 2 * pairs:2]
    margin = jnp.minimum(source_of - 1, reach - sink)
    shifted = jax.random.randint(jax.random.fold_in(rng, 1), (pairs,), 0, 1 << 20) % (margin + 1)
    sizes = sizes.at[1:1 + 2 * pairs:2].set(source_of - shifted).at[2:2 + 2 * pairs:2].set(sink + shifted)
    return sizes[jax.random.permutation(jax.random.fold_in(rng, 2), amount)]


def noise(key, dims, scale, most, shards=(), kind=jnp.bfloat16):
    gain = block_scale(key, dims, shards, -0.22, 0.18) if shards else 1.0
    values = jax.random.normal(key, dims, jnp.float32) * scale * gain
    return jnp.minimum(jnp.maximum(values, -most), most).astype(kind)


def noise_with(key, extent, scale, bound, cuts, heavy, kind=jnp.bfloat16):
    array = scale * jax.random.normal(key, extent, jnp.float32)
    if cuts:
        array = array * block_scale(key, extent, cuts, -0.22, 0.18)
    return jnp.clip(strengthened(array, jax.random.fold_in(key, 3), *heavy), -bound, bound).astype(kind)


def setup_inputs(seed: int = 0) -> dict:
    key_list = jax.random.split(jax.random.key(seed), 5)
    return {
        "design": noise_with(key_list[0], (ROWS, G), ROWS ** -0.5, 0.125, ((0, 8), (1, 4)), (0, 1, 8, 2.0)),
        "local_design": noise(key_list[1], (ROWS, LOCAL), CAP ** -0.5, 0.3125, ((0, 8),)),
        "lengths": uneven_parts(key_list[2], ARCS, ARCS * CAP * 3 // 4, CAP, 2).astype(jnp.int32),
        "regularizer": jnp.clip(jnp.exp(math.log(2.0) - 2.3025851 * jax.random.uniform(key_list[3], (G,), jnp.float32) ** block_scale(key_list[3], (G,), ((0, 32),), -0.2, 0.2)), 0.2, 2.0),
    }


ridge = 0.1

def reference(design, local_design, lengths, regularizer):
    arc_blocks = design.reshape(ARCS, CAP, G)
    local_cols = local_design.reshape(ARCS, CAP, LOCAL)
    live_rows = jnp.arange(CAP, dtype=jnp.int32)[None, :] < lengths[:, None]
    arc_blocks = jnp.where(live_rows[:, :, None], arc_blocks, jnp.zeros((), design.dtype))
    local_cols = jnp.where(live_rows[:, :, None], local_cols, jnp.zeros((), local_design.dtype)).astype(jnp.float32)
    local_normal = jnp.einsum('acl,acm->alm', local_cols, local_cols)
    local_normal = local_normal + ridge * jnp.eye(LOCAL, dtype=jnp.float32)[None]
    local_factor = jnp.linalg.cholesky(local_normal)
    basis_rows = lax.linalg.triangular_solve(local_factor, jnp.transpose(local_cols, (0, 2, 1)), left_side=True, lower=True)
    basis_rows = basis_rows.astype(jnp.bfloat16)
    basis_wide = basis_rows.astype(jnp.float32)
    loadings = jnp.einsum('alc,acw->alw', basis_wide, arc_blocks.astype(jnp.float32)).astype(jnp.bfloat16)
    cleaned = arc_blocks.astype(jnp.float32) - jnp.einsum('alc,alw->acw', basis_wide, loadings.astype(jnp.float32))
    flat_rows = cleaned.astype(jnp.bfloat16).reshape(ROWS, G)
    normal_work = jnp.dot(flat_rows.T.astype(jnp.float32), flat_rows.astype(jnp.float32), preferred_element_type=jnp.float32) + jnp.diag(regularizer)
    row_ids = jnp.arange(G, dtype=jnp.int32)
    panel_factors = []
    for panel_index in range(PANELS):
        lead_col = panel_index * PANEL
        panel_strip = normal_work[lead_col:lead_col + PANEL, :]
        lower_factor = jnp.linalg.cholesky(panel_strip[:, lead_col:lead_col + PANEL])
        col_factor = lax.linalg.triangular_solve(lower_factor, panel_strip, left_side=True, lower=True).T
        col_factor = jnp.where(row_ids[:, None] >= lead_col, col_factor, jnp.zeros((), jnp.float32))
        normal_work = normal_work - jnp.dot(col_factor, col_factor.T, precision=lax.Precision.HIGHEST)
        panel_factors.append(col_factor)
    return (normal_work, jnp.stack(panel_factors))
```

```python
import functools

import jax
import jax.numpy as jnp
from jax import lax
from jax.experimental import pallas as pl
from jax.experimental.pallas import tpu as pltpu
from jax.sharding import PartitionSpec as P

PANEL = 512
PANELS = 2
LEAD = PANEL * PANELS
RIDGE = 0.1
BLOCK = 128
HIGHEST = lax.Precision.HIGHEST
AXES = ("arc", "trow", "tcol")


def spread(value):
    return jnp.broadcast_to(value, (8, 128))


def small_inverse(pivot):
    d = [list(row) for row in pivot]
    low = [[None] * 8 for _ in range(8)]
    root = [None] * 8
    for k in range(8):
        root[k] = lax.rsqrt(d[k][k])
        for i in range(k + 1, 8):
            low[i][k] = d[i][k] * root[k]
        for j in range(k + 1, 8):
            for i in range(j, 8):
                d[i][j] = d[i][j] - low[i][k] * low[j][k]
    inv = [[None] * 8 for _ in range(8)]
    for k in range(8):
        inv[k][k] = root[k]
        for i in range(k + 1, 8):
            acc = low[i][k] * inv[k][k]
            for m in range(k + 1, i):
                acc = acc + low[i][m] * inv[m][k]
            inv[i][k] = -acc * root[i]
    return inv


def inverse_factors(matrices):
    lane = lax.broadcasted_iota(jnp.int32, (8, 128), 1)
    sub = lax.broadcasted_iota(jnp.int32, (8, 128), 0)
    zero = jnp.zeros((8, 128), jnp.float32)
    work = [[m[8 * i : 8 * i + 8, :] for i in range(16)] for m in matrices]
    unit = [
        [jnp.where(lane == sub + 8 * i, 1.0, 0.0).astype(jnp.float32) for i in range(16)]
        for _ in matrices
    ]
    for t in range(16):
        for A, X in zip(work, unit):
            lead = 8 * t
            cols = [spread(A[t][:, lead + k : lead + k + 1]) for k in range(8)]
            pivot = [
                [spread(cols[k][i : i + 1, :]) if k <= i else None for k in range(8)]
                for i in range(8)
            ]
            inv = small_inverse(pivot)
            U, UX = zero, zero
            for k in range(8):
                c = zero
                for i in range(k, 8):
                    c = jnp.where(sub == i, inv[i][k], c)
                U = U + c * spread(A[t][k : k + 1, :])
                UX = UX + c * spread(X[t][k : k + 1, :])
            X[t] = UX
            if t == 15:
                continue
            V, VX = zero, zero
            for m in range(8):
                c = zero
                for k in range(m + 1):
                    c = jnp.where(sub == k, inv[m][k], c)
                V = V + c * spread(U[m : m + 1, :])
                VX = VX + c * spread(UX[m : m + 1, :])
            rows = [spread(V[k : k + 1, :]) for k in range(8)]
            rows_x = [spread(VX[k : k + 1, :]) for k in range(8)]
            for i in range(t + 1, 16):
                cs = [spread(A[i][:, lead + k : lead + k + 1]) for k in range(8)]
                for k in range(8):
                    A[i] = A[i] - cs[k] * rows[k]
                    X[i] = X[i] - cs[k] * rows_x[k]
    return [jnp.concatenate(X, 0) for X in unit]


def basis_kernel(lengths_ref, local_ref, basis_ref):
    arcs = basis_ref.shape[0]
    capacity = basis_ref.shape[2]
    row = lax.broadcasted_iota(jnp.int32, (capacity, BLOCK), 0)
    eye = (
        lax.broadcasted_iota(jnp.int32, (BLOCK, BLOCK), 0)
        == lax.broadcasted_iota(jnp.int32, (BLOCK, BLOCK), 1)
    )
    masked, normals = [], []
    for a in range(arcs):
        block = local_ref[a * capacity : (a + 1) * capacity, :].astype(jnp.float32)
        block = jnp.where(row < lengths_ref[a], block, 0.0)
        half = block.astype(jnp.bfloat16)
        normal = lax.dot_general(
            half, half, (((0,), (0,)), ((), ())), preferred_element_type=jnp.float32
        )
        masked.append(block)
        normals.append(normal + jnp.where(eye, RIDGE, 0.0))
    for a, inverse in enumerate(inverse_factors(normals)):
        basis = lax.dot_general(
            inverse,
            masked[a],
            (((1,), (1,)), ((), ())),
            precision=HIGHEST,
            preferred_element_type=jnp.float32,
        )
        basis_ref[a] = basis.astype(jnp.bfloat16)


def local_basis(local_design, lengths):
    arcs = lengths.shape[0]
    capacity = local_design.shape[0] // arcs
    return pl.pallas_call(
        basis_kernel,
        out_shape=jax.ShapeDtypeStruct((arcs, BLOCK, capacity), jnp.bfloat16),
        in_specs=[
            pl.BlockSpec(memory_space=pltpu.SMEM),
            pl.BlockSpec(memory_space=pltpu.VMEM),
        ],
        out_specs=pl.BlockSpec(memory_space=pltpu.VMEM),
        compiler_params=pltpu.CompilerParams(vmem_limit_bytes=32 * 1024 * 1024),
        cost_estimate=pl.CostEstimate(flops=10**9, bytes_accessed=30_000_000, transcendentals=0),
        name="local_basis",
    )(lengths, local_design)


def lead_kernel(pivot_ref, out_ref):
    size = out_ref.shape[0]
    out_ref[...] = pivot_ref[...]
    blocks = size // BLOCK
    for k in range(blocks):
        here = slice(k * BLOCK, (k + 1) * BLOCK)
        inverse = inverse_factors([out_ref[here, here]])[0]
        lead_row = jnp.dot(
            inverse, out_ref[here, :], precision=HIGHEST, preferred_element_type=jnp.float32
        )
        below = slice((k + 1) * BLOCK, size)
        out_ref[here, :] = lead_row
        out_ref[here, here] = inverse
        if k + 1 < blocks:
            coef = out_ref[here, below]
            out_ref[below, here] = jnp.zeros((size - (k + 1) * BLOCK, BLOCK), jnp.float32)
            out_ref[below, :] = out_ref[below, :] - lax.dot_general(
                coef,
                out_ref[here, :],
                (((0,), (0,)), ((), ())),
                precision=HIGHEST,
                preferred_element_type=jnp.float32,
            )
            out_ref[here, below] = jnp.zeros((BLOCK, size - (k + 1) * BLOCK), jnp.float32)


def lead_inverse(pivot):
    return pl.pallas_call(
        lead_kernel,
        out_shape=jax.ShapeDtypeStruct(pivot.shape, jnp.float32),
        in_specs=[pl.BlockSpec(memory_space=pltpu.VMEM)],
        out_specs=pl.BlockSpec(memory_space=pltpu.VMEM),
        compiler_params=pltpu.CompilerParams(vmem_limit_bytes=48 * 1024 * 1024),
        cost_estimate=pl.CostEstimate(
            flops=80 * 10**9, bytes_accessed=250_000_000, transcendentals=0
        ),
        name="lead_inverse",
    )(pivot)


def project(rows, basis, live):
    arcs, _, capacity = basis.shape
    blocks = rows.reshape(arcs, capacity, rows.shape[1])
    loadings = jnp.einsum(
        "alc,acw->alw", basis, blocks, preferred_element_type=jnp.float32
    ).astype(jnp.bfloat16)
    cleaned = blocks.astype(jnp.float32) - jnp.einsum(
        "alc,alw->acw", basis, loadings, preferred_element_type=jnp.float32
    )
    cleaned = jnp.where(live[:, :, None], cleaned, 0.0)
    return cleaned.astype(jnp.bfloat16).reshape(rows.shape)


def contract_rows(left_rows, right_rows):
    return lax.dot_general(
        left_rows, right_rows, (((0,), (0,)), ((), ())), preferred_element_type=jnp.float32
    )


def per_device(design, local_design, lengths, regularizer):
    row_count, col_width = design.shape
    tile = regularizer.shape[0]
    arc_total = lax.axis_size("arc")
    trow_total = lax.axis_size("trow")
    tcol_total = lax.axis_size("tcol")
    arc = lax.axis_index("arc")
    trow = lax.axis_index("trow")
    tcol = lax.axis_index("tcol")
    arcs_per_col = arc_total // tcol_total
    capacity = row_count // lengths.shape[0]
    share = tile // arc_total

    def device_number(a, r, c):
        return (a * trow_total + r) * tcol_total + c

    def over_arc(step, columns):
        return [
            (device_number(a, r, c), device_number(a ^ step, r, c))
            for a in range(arc_total)
            for r in range(trow_total)
            for c in columns
        ]

    every = range(tcol_total)
    live = jnp.arange(capacity, dtype=jnp.int32)[None, :] < lengths[:, None]

    piece = lax.dynamic_slice_in_dim(
        design.reshape(row_count, arcs_per_col, trow_total, tile), trow, 1, 2
    ).reshape(row_count, arcs_per_col * tile)
    gathered = lax.all_gather(piece, "tcol", axis=0)

    basis = local_basis(local_design, lengths)
    own = project(design, basis, live)

    row_ids = jnp.arange(tile, dtype=jnp.int32)
    lead_rows = trow * tile + row_ids
    lead_reg = jnp.where(arc == 0, regularizer, 0.0)

    lead_cols = jnp.arange(LEAD, dtype=jnp.int32)
    pivot_part = contract_rows(
        lax.dynamic_slice_in_dim(own, trow * tile, tile, 1), own[:, :LEAD]
    ) + jnp.where(lead_rows[:, None] == lead_cols[None, :], lead_reg[:, None], 0.0)

    def scatter_sum(part, columns):
        total = lax.dynamic_slice_in_dim(part, arc * share, share, 0)
        for step in range(1, arc_total):
            piece = lax.dynamic_slice_in_dim(part, (arc ^ step) * share, share, 0)
            total = total + lax.ppermute(piece, AXES, over_arc(step, columns))
        return total

    pivot_share = scatter_sum(pivot_part, [0])
    spread_share = jnp.where(tcol == 0, pivot_share, 0.0)
    for c in range(1, tcol_total):
        spread_share = spread_share + lax.ppermute(
            pivot_share,
            AXES,
            [
                (device_number(a, r, 0), device_number(a, r, c))
                for a in range(arc_total)
                for r in range(trow_total)
            ],
        )

    def natural(gathered_rows):
        return (
            gathered_rows.reshape(arc_total, trow_total, share, gathered_rows.shape[-1])
            .transpose(1, 0, 2, 3)
            .reshape(LEAD, gathered_rows.shape[-1])
        )

    pivot = natural(lax.all_gather(spread_share, ("arc", "trow"), axis=0))
    inverse = lead_inverse(pivot)

    cross = gathered.transpose(1, 0, 2).reshape(row_count, arc_total * tile)
    cross = project(cross, basis, live)

    col_ids = tcol * col_width + jnp.arange(col_width, dtype=jnp.int32)
    strip_part = contract_rows(cross[:, :tile], own) + jnp.where(
        lead_rows[:, None] == col_ids[None, :], lead_reg[:, None], 0.0
    )
    strip_share = scatter_sum(strip_part, every)
    strip = natural(lax.all_gather(strip_share, ("arc", "trow"), axis=0))

    def tile_for(target):
        return contract_rows(lax.dynamic_slice_in_dim(cross, target * tile, tile, 1), own)

    normal = tile_for(arc)
    for step in range(1, arc_total):
        normal = normal + lax.ppermute(
            tile_for(arc ^ step).astype(jnp.bfloat16), AXES, over_arc(step, every)
        ).astype(jnp.float32)
    rows_global = (arc * trow_total + trow) * tile + row_ids
    normal = normal + jnp.where(
        rows_global[:, None] == col_ids[None, :], regularizer[:, None], 0.0
    )

    holder = arc // arcs_per_col
    row_own = lax.dynamic_slice_in_dim(
        strip, ((arc % arcs_per_col) * trow_total + trow) * tile, tile, 1
    )
    row_strip = jnp.where(tcol == holder, row_own, 0.0)
    for step in range(1, tcol_total):
        row_strip = row_strip + lax.ppermute(
            row_own,
            AXES,
            [
                (
                    device_number(a, r, a // arcs_per_col),
                    device_number(a, r, (a // arcs_per_col) ^ step),
                )
                for a in range(arc_total)
                for r in range(trow_total)
            ],
        )

    def factor_of(columns, ids):
        factors = []
        for p in range(PANELS):
            depth = (p + 1) * PANEL
            factor = lax.dot_general(
                columns[:depth],
                inverse[p * PANEL : depth, :depth],
                (((0,), (1,)), ((), ())),
                precision=lax.Precision.HIGH,
                preferred_element_type=jnp.float32,
            )
            factors.append(jnp.where(ids[:, None] >= p * PANEL, factor, 0.0))
        return factors

    col_factors = factor_of(strip, col_ids)
    row_factors = factor_of(row_strip, rows_global)
    for p in range(PANELS):
        normal = normal - lax.dot_general(
            row_factors[p],
            col_factors[p],
            (((1,), (1,)), ((), ())),
            precision=lax.Precision.HIGH,
            preferred_element_type=jnp.float32,
        )
    return normal, jnp.stack(col_factors)


def solution(mesh):
    return jax.shard_map(
        per_device,
        mesh=mesh,
        in_specs=(P("arc", "tcol"), P("arc", None), P("arc"), P(("arc", "trow"))),
        out_specs=(P(("arc", "trow"), "tcol"), P(None, "tcol", None)),
        check_vma=False,
    )
```

```python
import jax
import jax.numpy as jnp
from jax import lax
from jax.experimental import pallas as pl
from jax.experimental.pallas import tpu as pltpu
from jax.sharding import PartitionSpec as P

PANEL = 512
PANELS = 2
LEAD = PANEL * PANELS
RIDGE = 0.1
BLOCK = 128
HIGHEST = lax.Precision.HIGHEST
AXES = ("arc", "trow", "tcol")


def spread(value):
    return jnp.broadcast_to(value, (8, 128))


def small_inverse(pivot):
    d = [list(row) for row in pivot]
    low = [[None] * 8 for _ in range(8)]
    root = [None] * 8
    for k in range(8):
        root[k] = lax.rsqrt(d[k][k])
        for i in range(k + 1, 8):
            low[i][k] = d[i][k] * root[k]
        for j in range(k + 1, 8):
            for i in range(j, 8):
                d[i][j] = d[i][j] - low[i][k] * low[j][k]
    inv = [[None] * 8 for _ in range(8)]
    for k in range(8):
        inv[k][k] = root[k]
        for i in range(k + 1, 8):
            acc = low[i][k] * inv[k][k]
            for m in range(k + 1, i):
                acc = acc + low[i][m] * inv[m][k]
            inv[i][k] = -acc * root[i]
    return inv


def inverse_factors(matrices):
    lane = lax.broadcasted_iota(jnp.int32, (8, 128), 1)
    sub = lax.broadcasted_iota(jnp.int32, (8, 128), 0)
    zero = jnp.zeros((8, 128), jnp.float32)
    work = [[m[8 * i : 8 * i + 8, :] for i in range(16)] for m in matrices]
    unit = [
        [jnp.where(lane == sub + 8 * i, 1.0, 0.0).astype(jnp.float32) for i in range(16)]
        for _ in matrices
    ]
    for t in range(16):
        for A, X in zip(work, unit):
            lead = 8 * t
            cols = [spread(A[t][:, lead + k : lead + k + 1]) for k in range(8)]
            pivot = [
                [spread(cols[k][i : i + 1, :]) if k <= i else None for k in range(8)]
                for i in range(8)
            ]
            inv = small_inverse(pivot)
            U, UX = zero, zero
            for k in range(8):
                c = zero
                for i in range(k, 8):
                    c = jnp.where(sub == i, inv[i][k], c)
                U = U + c * spread(A[t][k : k + 1, :])
                UX = UX + c * spread(X[t][k : k + 1, :])
            X[t] = UX
            if t == 15:
                continue
            V, VX = zero, zero
            for m in range(8):
                c = zero
                for k in range(m + 1):
                    c = jnp.where(sub == k, inv[m][k], c)
                V = V + c * spread(U[m : m + 1, :])
                VX = VX + c * spread(UX[m : m + 1, :])
            rows = [spread(V[k : k + 1, :]) for k in range(8)]
            rows_x = [spread(VX[k : k + 1, :]) for k in range(8)]
            for i in range(t + 1, 16):
                cs = [spread(A[i][:, lead + k : lead + k + 1]) for k in range(8)]
                for k in range(8):
                    A[i] = A[i] - cs[k] * rows[k]
                    X[i] = X[i] - cs[k] * rows_x[k]
    return [jnp.concatenate(X, 0) for X in unit]


def basis_kernel(lengths_ref, local_ref, basis_ref):
    arcs = basis_ref.shape[0]
    capacity = basis_ref.shape[2]
    row = lax.broadcasted_iota(jnp.int32, (capacity, BLOCK), 0)
    eye = (
        lax.broadcasted_iota(jnp.int32, (BLOCK, BLOCK), 0)
        == lax.broadcasted_iota(jnp.int32, (BLOCK, BLOCK), 1)
    )
    masked, normals = [], []
    for a in range(arcs):
        block = local_ref[a * capacity : (a + 1) * capacity, :].astype(jnp.float32)
        block = jnp.where(row < lengths_ref[a], block, 0.0)
        half = block.astype(jnp.bfloat16)
        normal = lax.dot_general(
            half, half, (((0,), (0,)), ((), ())), preferred_element_type=jnp.float32
        )
        masked.append(block)
        normals.append(normal + jnp.where(eye, RIDGE, 0.0))
    for a, inverse in enumerate(inverse_factors(normals)):
        basis = lax.dot_general(
            inverse,
            masked[a],
            (((1,), (1,)), ((), ())),
            precision=HIGHEST,
            preferred_element_type=jnp.float32,
        )
        basis_ref[a] = basis.astype(jnp.bfloat16)


def local_basis(local_design, lengths):
    arcs = lengths.shape[0]
    capacity = local_design.shape[0] // arcs
    return pl.pallas_call(
        basis_kernel,
        out_shape=jax.ShapeDtypeStruct((arcs, BLOCK, capacity), jnp.bfloat16),
        in_specs=[
            pl.BlockSpec(memory_space=pltpu.SMEM),
            pl.BlockSpec(memory_space=pltpu.VMEM),
        ],
        out_specs=pl.BlockSpec(memory_space=pltpu.VMEM),
        compiler_params=pltpu.CompilerParams(vmem_limit_bytes=32 * 1024 * 1024),
        cost_estimate=pl.CostEstimate(flops=10**9, bytes_accessed=30_000_000, transcendentals=0),
        name="local_basis",
    )(lengths, local_design)


def mesh_copy(src, dst, send, recv, device):
    return pltpu.make_async_remote_copy(
        src_ref=src,
        dst_ref=dst,
        send_sem=send,
        recv_sem=recv,
        device_id=device,
        device_id_type=pl.DeviceIdType.MESH,
    )


def greet(devices):
    barrier = pltpu.get_barrier_semaphore()
    for device in devices:
        pl.semaphore_signal(
            barrier, inc=1, device_id=device, device_id_type=pl.DeviceIdType.MESH
        )
    pl.semaphore_wait(barrier, len(devices))


def reduce_kernel(
    pivot_part, strip_part, strip_out, pivot_out, pivot_in, strip_in, chunk, half, stack,
    part_send, part_recv, half_send, half_recv, stack_send, stack_recv,
    lead_send, lead_recv, core_send, core_recv, strip_send, strip_recv,
):
    trows, arcs, cores, depth, width = pivot_out.shape
    share = strip_out.shape[0]
    tcols = half_send.shape[0]
    tile = width // trows
    a, r, c = lax.axis_index("arc"), lax.axis_index("trow"), lax.axis_index("tcol")
    core = lax.rem(c, 2)
    greet(
        [(a ^ m, r, c) for m in range(1, arcs)]
        + [(a, r ^ q, c) for q in range(1, trows)]
        + [(a, r, c ^ q) for q in range(1, tcols)]
    )

    def rows_of(part, target):
        return part.at[pl.ds(pl.multiple_of(target * share, share), share)]

    @pl.when(c == 0)
    def _():
        copies = [
            mesh_copy(
                rows_of(pivot_part, a ^ m), pivot_in.at[m],
                part_send.at[m], part_recv.at[m], (a ^ m, r, c),
            )
            for m in range(1, arcs)
        ]
        for copy in copies:
            copy.start()
        total = rows_of(pivot_part, a)[...]
        for m, copy in enumerate(copies):
            copy.wait_recv()
            total = total + pivot_in[m + 1]
        chunk[...] = total.reshape(chunk.shape)
        spreads = [
            mesh_copy(chunk.at[q % 2], half, half_send.at[q], half_recv, (a, r, q))
            for q in range(1, tcols)
        ]
        for copy in spreads:
            copy.start()
        half[...] = chunk[0]
        for copy in copies + spreads:
            copy.wait_send()

    @pl.when(c != 0)
    def _():
        mesh_copy(chunk.at[0], half, half_send.at[0], half_recv, (a, r, c ^ 1)).wait_recv()

    stacked = [
        mesh_copy(half, stack.at[r], stack_send.at[q], stack_recv.at[q], (a, r ^ q, c))
        for q in range(1, trows)
    ]
    for copy in stacked:
        copy.start()
    stack[r] = half[...]
    for copy in stacked:
        copy.wait_recv()

    def columns(t):
        return pl.ds(t * tile, width - t * tile)

    leads = [
        [
            mesh_copy(
                stack.at[t, :, columns(t)], pivot_out.at[t, a, core, :, columns(t)],
                lead_send.at[m, t], lead_recv.at[m, t], (a ^ m, r, c),
            )
            for m in range(1, arcs)
        ]
        for t in range(trows)
    ]
    for group in leads:
        for copy in group:
            copy.start()
    strips = [
        mesh_copy(
            rows_of(strip_part, a ^ m), strip_in.at[m],
            strip_send.at[m], strip_recv.at[m], (a ^ m, r, c),
        )
        for m in range(1, arcs)
    ]
    for copy in strips:
        copy.start()
    for t in range(trows):
        pivot_out[t, a, core] = stack[t]
    others = []
    for t in range(trows):
        for copy in leads[t]:
            copy.wait_recv()
        copy = mesh_copy(
            pivot_out.at[t, :, core, :, columns(t)], pivot_out.at[t, :, core, :, columns(t)],
            core_send.at[t], core_recv.at[t], (a, r, c ^ 1),
        )
        copy.start()
        others.append(copy)
    total = rows_of(strip_part, a)[...]
    for m, copy in enumerate(strips):
        copy.wait_recv()
        total = total + strip_in[m + 1]
    strip_out[...] = total
    for copy in others:
        copy.wait()
    for copy in stacked + strips + [copy for group in leads for copy in group]:
        copy.wait_send()


def reduce_lead(pivot_part, strip_part, arcs, trows, tcols):
    tile, width = pivot_part.shape
    share = tile // arcs
    depth = share // 2
    dma = pltpu.SemaphoreType.DMA
    vmem = pl.BlockSpec(memory_space=pltpu.VMEM)
    return pl.pallas_call(
        reduce_kernel,
        out_shape=(
            jax.ShapeDtypeStruct((share, strip_part.shape[1]), jnp.float32),
            jax.ShapeDtypeStruct((trows, arcs, 2, depth, width), jnp.float32),
        ),
        in_specs=[vmem, vmem],
        out_specs=(vmem, vmem),
        scratch_shapes=[
            pltpu.VMEM((arcs, share, width), jnp.float32),
            pltpu.VMEM((arcs, share, strip_part.shape[1]), jnp.float32),
            pltpu.VMEM((2, depth, width), jnp.float32),
            pltpu.VMEM((depth, width), jnp.float32),
            pltpu.VMEM((trows, depth, width), jnp.float32),
            dma((arcs,)), dma((arcs,)),
            dma((tcols,)), dma,
            dma((trows,)), dma((trows,)),
            dma((arcs, trows)), dma((arcs, trows)),
            dma((trows,)), dma((trows,)),
            dma((arcs,)), dma((arcs,)),
        ],
        compiler_params=pltpu.CompilerParams(
            collective_id=0, has_side_effects=True, vmem_limit_bytes=32 * 1024 * 1024
        ),
        cost_estimate=pl.CostEstimate(
            flops=40 * 10**9, bytes_accessed=100_000_000, transcendentals=0
        ),
        name="reduce_lead",
    )(pivot_part, strip_part)


def eliminate(pivot_ref, out_ref):
    size = out_ref.shape[0]
    blocks = size // BLOCK
    out_ref[...] = pivot_ref[...]
    col = lax.broadcasted_iota(jnp.int32, (BLOCK, size), 1)

    def step(k, _):
        base = pl.multiple_of(k * BLOCK, BLOCK)
        here = pl.ds(base, BLOCK)
        after = base + BLOCK
        inverse = inverse_factors([out_ref[here, here]])[0]
        out_ref[here, here] = jnp.where(
            lax.broadcasted_iota(jnp.int32, (BLOCK, BLOCK), 0)
            == lax.broadcasted_iota(jnp.int32, (BLOCK, BLOCK), 1),
            1.0,
            0.0,
        )
        lead_row = jnp.dot(
            inverse, out_ref[here, :], precision=HIGHEST, preferred_element_type=jnp.float32
        )
        coef = jnp.where(col >= after, lead_row, 0.0)

        def trail(first):
            below = slice(first, size)
            row = lax.broadcasted_iota(jnp.int32, (size - first, BLOCK), 0) + first
            out_ref[below, here] = jnp.where(row >= after, 0.0, out_ref[below, here])
            out_ref[below, :] = out_ref[below, :] - lax.dot_general(
                coef[:, below],
                lead_row,
                (((0,), (0,)), ((), ())),
                precision=HIGHEST,
                preferred_element_type=jnp.float32,
            )

        half = blocks // 2

        @pl.when(k < half)
        def _():
            trail(BLOCK)

        @pl.when((k >= half) & (k < blocks - 1))
        def _():
            trail((half + 1) * BLOCK)

        out_ref[here, :] = jnp.where(col < after, lead_row, 0.0)
        return 0

    lax.fori_loop(0, blocks, step, 0)


def exchange_kernel(pivot_ref, tiles, inverse_ref, received, send, recv):
    arcs = tiles.shape[0]
    a, r, c = lax.axis_index("arc"), lax.axis_index("trow"), lax.axis_index("tcol")
    greet([(a ^ m, r, c) for m in range(1, arcs)])
    copies = [
        mesh_copy(
            tiles.at[a ^ m], received.at[m - 1], send.at[m - 1], recv.at[m - 1], (a ^ m, r, c)
        )
        for m in range(1, arcs)
    ]
    for copy in copies:
        copy.start()
    eliminate(pivot_ref, inverse_ref)
    for copy in copies:
        copy.wait()


def exchange_and_eliminate(pivot, tiles):
    arcs = tiles.shape[0]
    return pl.pallas_call(
        exchange_kernel,
        out_shape=(
            jax.ShapeDtypeStruct(pivot.shape, jnp.float32),
            jax.ShapeDtypeStruct((arcs - 1,) + tiles.shape[1:], tiles.dtype),
        ),
        in_specs=[
            pl.BlockSpec(memory_space=pltpu.VMEM),
            pl.BlockSpec(memory_space=pl.ANY),
        ],
        out_specs=(
            pl.BlockSpec(memory_space=pltpu.VMEM),
            pl.BlockSpec(memory_space=pl.ANY),
        ),
        scratch_shapes=[
            pltpu.SemaphoreType.DMA((arcs - 1,)),
            pltpu.SemaphoreType.DMA((arcs - 1,)),
        ],
        compiler_params=pltpu.CompilerParams(
            collective_id=1, has_side_effects=True, vmem_limit_bytes=48 * 1024 * 1024
        ),
        cost_estimate=pl.CostEstimate(
            flops=80 * 10**9, bytes_accessed=350_000_000, transcendentals=0
        ),
        name="exchange_and_eliminate",
    )(pivot, tiles)


def project(rows, basis, live):
    arcs, _, capacity = basis.shape
    blocks = rows.reshape(rows.shape[0], arcs, capacity, rows.shape[2])
    loadings = jnp.einsum(
        "alc,tacw->talw", basis, blocks, preferred_element_type=jnp.float32
    ).astype(jnp.bfloat16)
    cleaned = blocks.astype(jnp.float32) - jnp.einsum(
        "alc,talw->tacw", basis, loadings, preferred_element_type=jnp.float32
    )
    cleaned = jnp.where(live[None, :, :, None], cleaned, 0.0)
    return cleaned.astype(jnp.bfloat16).reshape(rows.shape)


def contract_rows(left_rows, right_rows):
    return lax.dot_general(
        left_rows, right_rows, (((0,), (0,)), ((), ())), preferred_element_type=jnp.float32
    )


def per_device(design, local_design, lengths, regularizer):
    row_count, col_width = design.shape
    tile = regularizer.shape[0]
    arc_total = lax.axis_size("arc")
    trow_total = lax.axis_size("trow")
    tcol_total = lax.axis_size("tcol")
    arc = lax.axis_index("arc")
    trow = lax.axis_index("trow")
    tcol = lax.axis_index("tcol")
    arcs_per_col = arc_total // tcol_total
    capacity = row_count // lengths.shape[0]
    share = tile // arc_total

    def device_number(a, r, c):
        return (a * trow_total + r) * tcol_total + c

    live = jnp.arange(capacity, dtype=jnp.int32)[None, :] < lengths[:, None]

    piece = jnp.stack(
        [
            lax.dynamic_slice_in_dim(design, (e * trow_total + trow) * tile, tile, 1)
            for e in range(arcs_per_col)
        ]
    )
    gathered = lax.all_gather(piece, "tcol", axis=0, tiled=True)

    basis = local_basis(local_design, lengths)
    own = project(design[None], basis, live)[0]

    row_ids = jnp.arange(tile, dtype=jnp.int32)
    lead_rows = trow * tile + row_ids
    lead_reg = jnp.where(arc == 0, regularizer, 0.0)

    lead_cols = jnp.arange(LEAD, dtype=jnp.int32)
    pivot_part = contract_rows(
        lax.dynamic_slice_in_dim(own, trow * tile, tile, 1), own[:, :LEAD]
    ) + jnp.where(lead_rows[:, None] == lead_cols[None, :], lead_reg[:, None], 0.0)

    def natural(gathered_rows):
        return (
            gathered_rows.reshape(arc_total, trow_total, share, gathered_rows.shape[-1])
            .transpose(1, 0, 2, 3)
            .reshape(LEAD, gathered_rows.shape[-1])
        )

    cross = project(gathered, basis, live)

    col_ids = tcol * col_width + jnp.arange(col_width, dtype=jnp.int32)
    strip_part = contract_rows(cross[0], own) + jnp.where(
        lead_rows[:, None] == col_ids[None, :], lead_reg[:, None], 0.0
    )
    strip_share, pivot = reduce_lead(pivot_part, strip_part, arc_total, trow_total, tcol_total)
    pivot = pivot.reshape(LEAD, LEAD)
    strip = natural(lax.all_gather(strip_share, ("arc", "trow"), axis=0))

    tiles = jnp.einsum(
        "tnw,nv->twv", cross, own, preferred_element_type=jnp.float32
    ).astype(jnp.bfloat16)
    inverse, received = exchange_and_eliminate(pivot, tiles)
    normal = contract_rows(lax.dynamic_index_in_dim(cross, arc, 0, False), own)
    normal = normal + jnp.sum(received.astype(jnp.float32), axis=0)
    rows_global = (arc * trow_total + trow) * tile + row_ids
    normal = normal + jnp.where(
        rows_global[:, None] == col_ids[None, :], regularizer[:, None], 0.0
    )

    holder = arc // arcs_per_col
    row_own = lax.dynamic_slice_in_dim(
        strip, ((arc % arcs_per_col) * trow_total + trow) * tile, tile, 1
    )
    row_strip = jnp.where(tcol == holder, row_own, 0.0)
    for step in range(1, tcol_total):
        row_strip = row_strip + lax.ppermute(
            row_own,
            AXES,
            [
                (
                    device_number(a, r, a // arcs_per_col),
                    device_number(a, r, (a // arcs_per_col) ^ step),
                )
                for a in range(arc_total)
                for r in range(trow_total)
            ],
        )

    def factor_of(columns, ids):
        factors = []
        for p in range(PANELS):
            depth = (p + 1) * PANEL
            factor = lax.dot_general(
                columns[:depth],
                inverse[p * PANEL : depth, :depth],
                (((0,), (1,)), ((), ())),
                precision=lax.Precision.HIGH,
                preferred_element_type=jnp.float32,
            )
            factors.append(jnp.where(ids[:, None] >= p * PANEL, factor, 0.0))
        return factors

    col_factors = factor_of(strip, col_ids)
    row_factors = factor_of(row_strip, rows_global)
    for p in range(PANELS):
        normal = normal - lax.dot_general(
            row_factors[p],
            col_factors[p],
            (((1,), (1,)), ((), ())),
            precision=lax.Precision.HIGH,
            preferred_element_type=jnp.float32,
        )
    return normal, jnp.stack(col_factors)


def solution(mesh):
    return jax.shard_map(
        per_device,
        mesh=mesh,
        in_specs=(P("arc", "tcol"), P("arc", None), P("arc"), P(("arc", "trow"))),
        out_specs=(P(("arc", "trow"), "tcol"), P(None, "tcol", None)),
        check_vma=False,
    )
```

```python
import jax
import jax.numpy as jnp
from jax import lax
from jax.experimental import pallas as pl
from jax.experimental.pallas import tpu as pltpu
from jax.sharding import PartitionSpec as P

PANEL = 512
PANELS = 2
LEAD = PANEL * PANELS
RIDGE = 0.1
BLOCK = 128
HIGHEST = lax.Precision.HIGHEST
AXES = ("arc", "trow", "tcol")


def spread(value):
    return jnp.broadcast_to(value, (8, 128))


def small_inverse(pivot):
    d = [list(row) for row in pivot]
    low = [[None] * 8 for _ in range(8)]
    root = [None] * 8
    for k in range(8):
        root[k] = lax.rsqrt(d[k][k])
        for i in range(k + 1, 8):
            low[i][k] = d[i][k] * root[k]
        for j in range(k + 1, 8):
            for i in range(j, 8):
                d[i][j] = d[i][j] - low[i][k] * low[j][k]
    inv = [[None] * 8 for _ in range(8)]
    for k in range(8):
        inv[k][k] = root[k]
        for i in range(k + 1, 8):
            acc = low[i][k] * inv[k][k]
            for m in range(k + 1, i):
                acc = acc + low[i][m] * inv[m][k]
            inv[i][k] = -acc * root[i]
    return inv


def inverse_factors(matrices):
    lane = lax.broadcasted_iota(jnp.int32, (8, 128), 1)
    sub = lax.broadcasted_iota(jnp.int32, (8, 128), 0)
    zero = jnp.zeros((8, 128), jnp.float32)
    work = [[m[8 * i : 8 * i + 8, :] for i in range(16)] for m in matrices]
    unit = [
        [jnp.where(lane == sub + 8 * i, 1.0, 0.0).astype(jnp.float32) for i in range(16)]
        for _ in matrices
    ]
    for t in range(16):
        for A, X in zip(work, unit):
            lead = 8 * t
            cols = [spread(A[t][:, lead + k : lead + k + 1]) for k in range(8)]
            pivot = [
                [spread(cols[k][i : i + 1, :]) if k <= i else None for k in range(8)]
                for i in range(8)
            ]
            inv = small_inverse(pivot)
            U, UX = zero, zero
            for k in range(8):
                c = zero
                for i in range(k, 8):
                    c = jnp.where(sub == i, inv[i][k], c)
                U = U + c * spread(A[t][k : k + 1, :])
                UX = UX + c * spread(X[t][k : k + 1, :])
            X[t] = UX
            if t == 15:
                continue
            V, VX = zero, zero
            for m in range(8):
                c = zero
                for k in range(m + 1):
                    c = jnp.where(sub == k, inv[m][k], c)
                V = V + c * spread(U[m : m + 1, :])
                VX = VX + c * spread(UX[m : m + 1, :])
            rows = [spread(V[k : k + 1, :]) for k in range(8)]
            rows_x = [spread(VX[k : k + 1, :]) for k in range(8)]
            for i in range(t + 1, 16):
                cs = [spread(A[i][:, lead + k : lead + k + 1]) for k in range(8)]
                for k in range(8):
                    A[i] = A[i] - cs[k] * rows[k]
                    X[i] = X[i] - cs[k] * rows_x[k]
    return [jnp.concatenate(X, 0) for X in unit]


def basis_kernel(lengths_ref, local_ref, basis_ref):
    arcs = basis_ref.shape[0]
    capacity = basis_ref.shape[2]
    row = lax.broadcasted_iota(jnp.int32, (capacity, BLOCK), 0)
    eye = (
        lax.broadcasted_iota(jnp.int32, (BLOCK, BLOCK), 0)
        == lax.broadcasted_iota(jnp.int32, (BLOCK, BLOCK), 1)
    )
    masked, normals = [], []
    for a in range(arcs):
        block = local_ref[a * capacity : (a + 1) * capacity, :].astype(jnp.float32)
        block = jnp.where(row < lengths_ref[a], block, 0.0)
        half = block.astype(jnp.bfloat16)
        normal = lax.dot_general(
            half, half, (((0,), (0,)), ((), ())), preferred_element_type=jnp.float32
        )
        masked.append(block)
        normals.append(normal + jnp.where(eye, RIDGE, 0.0))
    for a, inverse in enumerate(inverse_factors(normals)):
        basis = lax.dot_general(
            inverse,
            masked[a],
            (((1,), (1,)), ((), ())),
            precision=HIGHEST,
            preferred_element_type=jnp.float32,
        )
        basis_ref[a] = basis.astype(jnp.bfloat16)


def local_basis(local_design, lengths):
    arcs = lengths.shape[0]
    capacity = local_design.shape[0] // arcs
    return pl.pallas_call(
        basis_kernel,
        out_shape=jax.ShapeDtypeStruct((arcs, BLOCK, capacity), jnp.bfloat16),
        in_specs=[
            pl.BlockSpec(memory_space=pltpu.SMEM),
            pl.BlockSpec(memory_space=pltpu.VMEM),
        ],
        out_specs=pl.BlockSpec(memory_space=pltpu.VMEM),
        compiler_params=pltpu.CompilerParams(vmem_limit_bytes=32 * 1024 * 1024),
        cost_estimate=pl.CostEstimate(flops=10**9, bytes_accessed=30_000_000, transcendentals=0),
        name="local_basis",
    )(lengths, local_design)


def mesh_copy(src, dst, send, recv, device):
    return pltpu.make_async_remote_copy(
        src_ref=src,
        dst_ref=dst,
        send_sem=send,
        recv_sem=recv,
        device_id=device,
        device_id_type=pl.DeviceIdType.MESH,
    )


def greet(devices):
    barrier = pltpu.get_barrier_semaphore()
    for device in devices:
        pl.semaphore_signal(
            barrier, inc=1, device_id=device, device_id_type=pl.DeviceIdType.MESH
        )
    pl.semaphore_wait(barrier, len(devices))


def eliminate(out_ref, before):
    size = out_ref.shape[0]
    blocks = size // BLOCK
    col = lax.broadcasted_iota(jnp.int32, (BLOCK, size), 1)

    def step(k, _):
        before(k)
        base = pl.multiple_of(k * BLOCK, BLOCK)
        here = pl.ds(base, BLOCK)
        after = base + BLOCK
        inverse = inverse_factors([out_ref[here, here]])[0]
        out_ref[here, here] = jnp.where(
            lax.broadcasted_iota(jnp.int32, (BLOCK, BLOCK), 0)
            == lax.broadcasted_iota(jnp.int32, (BLOCK, BLOCK), 1),
            1.0,
            0.0,
        )
        lead_row = jnp.dot(
            inverse, out_ref[here, :], precision=HIGHEST, preferred_element_type=jnp.float32
        )
        coef = jnp.where(col >= after, lead_row, 0.0)

        def trail(first):
            below = slice(first, size)
            row = lax.broadcasted_iota(jnp.int32, (size - first, BLOCK), 0) + first
            out_ref[below, here] = jnp.where(row >= after, 0.0, out_ref[below, here])
            out_ref[below, :] = out_ref[below, :] - lax.dot_general(
                coef[:, below],
                lead_row,
                (((0,), (0,)), ((), ())),
                precision=HIGHEST,
                preferred_element_type=jnp.float32,
            )

        half = blocks // 2

        @pl.when(k < half)
        def _():
            trail(BLOCK)

        @pl.when((k >= half) & (k < blocks - 1))
        def _():
            trail((half + 1) * BLOCK)

        out_ref[here, :] = jnp.where(col < after, lead_row, 0.0)
        return 0

    lax.fori_loop(0, blocks, step, 0)


def gather_kernel(
    own, piece, pivot_part, regs, pivot, strip_out, both, cross,
    pivot_in, strip_part, strip_in, chunk, half, stack, total_ref, first, swap_in, pair_sum, pair_in,
    first_send, first_recv, swap_send, swap_recv, mine_send, mine_recv,
    theirs_send, theirs_recv, plane_send, plane_recv,
    part_send, part_recv, half_send, half_recv, stack_send, stack_recv,
    lead_send, lead_recv, core_send, core_recv, strip_send, strip_recv,
    wide_send, wide_recv, relay_send, relay_recv, pair_send, pair_recv, own_sem, local_sem,
):
    trows, arcs, cores, depth, width = pivot.shape
    share = total_ref.shape[0]
    tcols = half_send.shape[0]
    tile = width // trows
    a, r, c = lax.axis_index("arc"), lax.axis_index("trow"), lax.axis_index("tcol")
    core = lax.rem(c, 2)
    parity = lax.rem(a, 2)
    others = range(1, arcs)
    greet(
        [(a ^ m, r, c) for m in others]
        + [(a, r ^ q, c) for q in range(1, trows)]
        + [(a, r, c ^ q) for q in range(1, tcols)]
    )

    def rows_of(part, target):
        return part.at[pl.ds(pl.multiple_of(target * share, share), share)]

    parts = [
        mesh_copy(
            rows_of(pivot_part, a ^ m), pivot_in.at[m],
            part_send.at[m], part_recv.at[m], (a ^ m, r, c),
        )
        for m in others
    ]
    groups = arcs // 2
    beyond = range(1, groups)
    strips = [
        mesh_copy(
            strip_part.at[pl.ds(pl.multiple_of((a // 2 ^ m) * 2 * share, 2 * share), 2 * share)],
            strip_in.at[m],
            strip_send.at[m], strip_recv.at[m], (a ^ (2 * m), r, c),
        )
        for m in beyond
    ]
    firsts = [
        mesh_copy(piece.at[0], first, first_send.at[q], first_recv, (a, r, q))
        for q in range(1, tcols)
    ]
    swap = mesh_copy(piece, swap_in, swap_send, swap_recv, (a ^ 1, r, c))
    mine = [
        mesh_copy(
            piece.at[parity], cross.at[c, 0], mine_send.at[q], mine_recv.at[q], (a, r, c ^ q)
        )
        for q in (1, 2)
    ]
    theirs = [
        mesh_copy(
            swap_in.at[parity], cross.at[c, 1], theirs_send.at[q], theirs_recv.at[q], (a, r, c ^ q)
        )
        for q in (1, 2)
    ]
    relays = [
        mesh_copy(
            cross.at[c ^ 2], cross.at[c ^ 2], relay_send.at[0], relay_recv.at[0], (a, r, c ^ 1)
        )
    ]

    def spot(e):
        return pl.ds(pl.multiple_of((e * trows + r) * tile, tile), tile)

    planes = [
        mesh_copy(
            swap_in.at[e], both.at[1, :, spot(e)],
            plane_send.at[q, e], plane_recv.at[q, e], (a, r ^ q, c),
        )
        for q in range(1, trows)
        for e in range(piece.shape[0])
    ]

    @pl.when(c == 0)
    def _():
        for copy in parts + firsts:
            copy.start()
        first[...] = piece[0]

    swap.start()
    keep_mine = pltpu.make_async_copy(piece.at[parity], cross.at[c, 0], local_sem.at[0])
    keep_mine.start()
    keep_own = pltpu.make_async_copy(own, both.at[0], local_sem.at[4])
    keep_own.start()
    for copy in mine:
        copy.start()

    @pl.when(c != 0)
    def _():
        mesh_copy(piece.at[0], first, first_send.at[0], first_recv, (a, r, c ^ 1)).wait_recv()

    wide = 512
    for j in range(0, own.shape[1], wide):
        strip_part[:, j : j + wide] = lax.dot_general(
            first[...],
            own[:, j : j + wide],
            (((0,), (0,)), ((), ())),
            preferred_element_type=jnp.float32,
        )
    lead = pl.ds(pl.multiple_of(r * tile, tile), tile)
    strip_part[:, lead] = strip_part[:, lead] + regs[...]
    for copy in strips:
        copy.start()

    @pl.when(c == 0)
    def _():
        total = rows_of(pivot_part, a)[...]
        for m, copy in enumerate(parts):
            copy.wait_recv()
            total = total + pivot_in[m + 1]
        chunk[...] = total.reshape(chunk.shape)
        spreads = [
            mesh_copy(chunk.at[q % 2], half, half_send.at[q], half_recv, (a, r, q))
            for q in range(1, tcols)
        ]
        for copy in spreads:
            copy.start()
        half[...] = chunk[0]
        for copy in parts + firsts + spreads:
            copy.wait_send()

    @pl.when(c != 0)
    def _():
        mesh_copy(chunk.at[0], half, half_send.at[0], half_recv, (a, r, c ^ 1)).wait_recv()

    stacked = [
        mesh_copy(half, stack.at[r], stack_send.at[q], stack_recv.at[q], (a, r ^ q, c))
        for q in range(1, trows)
    ]
    for copy in stacked:
        copy.start()
    stack[r] = half[...]
    swap.wait_recv()
    for copy in theirs + planes:
        copy.start()
    keep_theirs = pltpu.make_async_copy(swap_in.at[parity], cross.at[c, 1], local_sem.at[1])
    keep_planes = [
        pltpu.make_async_copy(swap_in.at[e], both.at[1, :, spot(e)], local_sem.at[2 + e])
        for e in range(piece.shape[0])
    ]
    for copy in [keep_theirs] + keep_planes:
        copy.start()
    for copy in stacked:
        copy.wait_recv()

    def columns(t):
        return pl.ds(t * tile, width - t * tile)

    leads = [
        [
            mesh_copy(
                stack.at[t, :, columns(t)], pivot.at[t, a, core, :, columns(t)],
                lead_send.at[m, t], lead_recv.at[m, t], (a ^ m, r, c),
            )
            for m in others
        ]
        for t in range(trows)
    ]
    for group in leads:
        for copy in group:
            copy.start()
    for t in range(trows):
        pivot[t, a, core] = stack[t]

    total = strip_part[pl.ds(pl.multiple_of(a // 2 * 2 * share, 2 * share), 2 * share)]
    for m, copy in enumerate(strips):
        copy.wait_recv()
        total = total + strip_in[m + 1]
    pair_sum[...] = total
    pair = mesh_copy(
        rows_of(pair_sum, 1 - parity), pair_in, pair_send, pair_recv, (a ^ 1, r, c)
    )
    pair.start()
    for copy in mine + theirs:
        copy.wait_recv()
    for copy in relays:
        copy.start()
    pair.wait_recv()
    total_ref[...] = rows_of(pair_sum, parity)[...] + pair_in[...]
    own_copy = pltpu.make_async_copy(total_ref, strip_out.at[a], own_sem)
    own_copy.start()
    wides = [
        mesh_copy(total_ref, strip_out.at[a], wide_send.at[m], wide_recv.at[m], (a ^ m, r, c))
        for m in [1] + [2 * m for m in beyond]
    ]
    for copy in wides:
        copy.start()
    wides[0].wait_recv()
    onward = [
        mesh_copy(
            strip_out.at[a ^ 1], strip_out.at[a ^ 1],
            relay_send.at[m], relay_recv.at[m], (a ^ (2 * m), r, c),
        )
        for m in beyond
    ]
    for copy in onward:
        copy.start()

    swaps = []
    for t in range(trows):
        for copy in leads[t]:
            copy.wait_recv()
        copy = mesh_copy(
            pivot.at[t, :, core, :, columns(t)], pivot.at[t, :, core, :, columns(t)],
            core_send.at[t], core_recv.at[t], (a, r, c ^ 1),
        )
        copy.start()
        swaps.append(copy)
    for copy in swaps + planes + relays + wides[1:] + onward:
        copy.wait()
    for copy in [keep_own, keep_mine, keep_theirs, own_copy] + keep_planes:
        copy.wait()
    sent = [swap, pair, wides[0]] + mine + theirs + stacked + strips
    for copy in sent + [copy for group in leads for copy in group]:
        copy.wait_send()


def gather(own, piece, pivot_part, regs, arcs, trows, tcols):
    tile, width = pivot_part.shape
    rows, columns = own.shape
    share = tile // arcs
    depth = share // 2
    dma = pltpu.SemaphoreType.DMA
    vmem = pl.BlockSpec(memory_space=pltpu.VMEM)
    anywhere = pl.BlockSpec(memory_space=pl.ANY)
    return pl.pallas_call(
        gather_kernel,
        out_shape=(
            jax.ShapeDtypeStruct((trows, arcs, 2, depth, width), jnp.float32),
            jax.ShapeDtypeStruct((arcs, share, columns), jnp.float32),
            jax.ShapeDtypeStruct((2,) + own.shape, own.dtype),
            jax.ShapeDtypeStruct((tcols, 2) + piece.shape[1:], piece.dtype),
        ),
        in_specs=[vmem] * 4,
        out_specs=(vmem, anywhere, anywhere, anywhere),
        scratch_shapes=[
            pltpu.VMEM((arcs, share, width), jnp.float32),
            pltpu.VMEM((tile, columns), jnp.float32),
            pltpu.VMEM((arcs // 2, 2 * share, columns), jnp.float32),
            pltpu.VMEM((2, depth, width), jnp.float32),
            pltpu.VMEM((depth, width), jnp.float32),
            pltpu.VMEM((trows, depth, width), jnp.float32),
            pltpu.VMEM((share, columns), jnp.float32),
            pltpu.VMEM(piece.shape[1:], piece.dtype),
            pltpu.VMEM(piece.shape, piece.dtype),
            pltpu.VMEM((2 * share, columns), jnp.float32),
            pltpu.VMEM((share, columns), jnp.float32),
            dma((tcols,)), dma,
            dma, dma,
            dma((tcols,)), dma((tcols,)),
            dma((tcols,)), dma((tcols,)),
            dma((trows, 2)), dma((trows, 2)),
            dma((arcs,)), dma((arcs,)),
            dma((tcols,)), dma,
            dma((trows,)), dma((trows,)),
            dma((arcs, trows)), dma((arcs, trows)),
            dma((trows,)), dma((trows,)),
            dma((arcs,)), dma((arcs,)),
            dma((arcs,)), dma((arcs,)),
            dma((arcs // 2,)), dma((arcs // 2,)),
            dma, dma,
            dma, dma((5,)),
        ],
        compiler_params=pltpu.CompilerParams(
            collective_id=0, has_side_effects=True, vmem_limit_bytes=40 * 1024 * 1024
        ),
        cost_estimate=pl.CostEstimate(
            flops=40 * 10**9, bytes_accessed=250_000_000, transcendentals=0
        ),
        name="gather",
    )(own, piece, pivot_part, regs)


def lead_kernel(
    pivot, plane, tiles, diagonals, inverse_ref, strip_out, received, diagonals_in, rows_out,
    near_send, near_recv, far_send, far_recv, tile_send, tile_recv, own_sem,
    diagonal_send, diagonal_recv, row_send, row_recv, row_local,
):
    trows, arcs = strip_out.shape[:2]
    groups = tiles.shape[0]
    a, r, c = lax.axis_index("arc"), lax.axis_index("trow"), lax.axis_index("tcol")
    up, down = lax.rem(r + 1, trows), lax.rem(r + trows - 1, trows)
    group = a // 2
    tcols = row_send.shape[1]
    tile = rows_out.shape[-1]
    greet(
        [(a ^ (2 * m), r, c) for m in range(1, groups)]
        + [(a, up, c), (a, down, c)]
        + [(a, r, c ^ q) for q in range(1, tcols)]
    )
    some = arcs // 2
    near = [
        mesh_copy(plane, strip_out.at[r], near_send.at[i], near_recv.at[i], (a, z, c))
        for i, z in enumerate((up, down))
    ]
    far = [
        mesh_copy(
            strip_out.at[z, part], strip_out.at[z, part],
            far_send.at[i], far_recv.at[i], (a, to, c),
        )
        for i, (z, part, to) in enumerate(
            ((down, pl.ds(0, some), up), (up, pl.ds(some, some), down))
        )
    ]
    exchanges = [
        mesh_copy(
            tiles.at[group ^ m], received.at[m - 1],
            tile_send.at[m - 1], tile_recv.at[m - 1], (a ^ (2 * m), r, c),
        )
        for m in range(1, groups)
    ] + [
        mesh_copy(
            diagonals.at[group ^ m], diagonals_in.at[m - 1],
            diagonal_send.at[m - 1], diagonal_recv.at[m - 1], (a ^ (2 * m), r, c),
        )
        for m in range(1, groups)
    ]

    holder = c == group
    spot = pl.ds(pl.multiple_of((lax.rem(a, 2) * trows + r) * tile, tile), tile)
    places = (r, up, down, lax.rem(r + 2, trows))

    def row_copies(i):
        source = (plane if i == 0 else strip_out.at[places[i]]).at[:, :, spot]
        target = rows_out.at[places[i]]
        away = [
            mesh_copy(source, target, row_send.at[i, q], row_recv.at[i], (a, r, c ^ q))
            for q in range(1, tcols)
        ]
        return away, pltpu.make_async_copy(source, target, row_local.at[i])

    def send_rows(i):
        @pl.when(holder)
        def _():
            away, here = row_copies(i)
            for copy in away:
                copy.start()
            here.start()

    send_rows(0)
    for copy in near + exchanges:
        copy.start()
    keep = pltpu.make_async_copy(plane, strip_out.at[r], own_sem)
    keep.start()
    inverse_ref[...] = pivot[...].reshape(inverse_ref.shape)

    def before(k):
        @pl.when(k == 6)
        def _():
            for copy in near:
                copy.wait_recv()
            for copy in far:
                copy.start()
            send_rows(1)
            send_rows(2)

    eliminate(inverse_ref, before)
    for copy in far:
        copy.wait_recv()
    send_rows(3)
    for copy in exchanges:
        copy.wait()

    @pl.when(holder)
    def _():
        for i in range(len(places)):
            away, here = row_copies(i)
            for copy in away:
                copy.wait_send()
            here.wait()

    @pl.when(jnp.logical_not(holder))
    def _():
        for i in range(len(places)):
            row_copies(i)[0][0].wait_recv()

    for copy in far:
        copy.wait_send()
    for copy in near:
        copy.wait_send()
    keep.wait()


def lead(pivot, plane, tiles, diagonals, tcols):
    trows, arcs = pivot.shape[:2]
    width = pivot.shape[-1]
    groups = tiles.shape[0]
    dma = pltpu.SemaphoreType.DMA
    vmem = pl.BlockSpec(memory_space=pltpu.VMEM)
    anywhere = pl.BlockSpec(memory_space=pl.ANY)
    return pl.pallas_call(
        lead_kernel,
        out_shape=(
            jax.ShapeDtypeStruct((width, width), jnp.float32),
            jax.ShapeDtypeStruct((trows,) + plane.shape, jnp.float32),
            jax.ShapeDtypeStruct((groups - 1,) + tiles.shape[1:], tiles.dtype),
            jax.ShapeDtypeStruct((groups - 1,) + diagonals.shape[1:], jnp.float32),
            jax.ShapeDtypeStruct((trows,) + plane.shape[:2] + diagonals.shape[2:], jnp.float32),
        ),
        in_specs=[vmem, anywhere, anywhere, vmem],
        out_specs=(vmem, anywhere, anywhere, vmem, anywhere),
        scratch_shapes=[
            dma((2,)), dma((2,)),
            dma((2,)), dma((2,)),
            dma((groups - 1,)), dma((groups - 1,)),
            dma,
            dma((groups - 1,)), dma((groups - 1,)),
            dma((trows, tcols)), dma((trows,)), dma((trows,)),
        ],
        compiler_params=pltpu.CompilerParams(
            collective_id=1, has_side_effects=True, vmem_limit_bytes=48 * 1024 * 1024
        ),
        cost_estimate=pl.CostEstimate(
            flops=80 * 10**9, bytes_accessed=250_000_000, transcendentals=0
        ),
        name="lead",
    )(pivot, plane, tiles, diagonals)


def halves(value):
    high = value.astype(jnp.bfloat16)
    return high, (value - high.astype(jnp.float32)).astype(jnp.bfloat16)


def factor_kernel(first_ref, strip_ref, high_ref, low_ref, out_ref):
    wide = strip_ref.shape[1]
    column = (
        first_ref[0] + pl.program_id(0) * wide
        + lax.broadcasted_iota(jnp.int32, (wide, PANEL), 0)
    )
    high, low = halves(strip_ref[...])

    def product(left, right):
        return lax.dot_general(
            left, right, (((0,), (0,)), ((), ())), preferred_element_type=jnp.float32
        )

    for p in range(PANELS):
        depth = (p + 1) * PANEL
        panel = slice(p * PANEL, depth)
        factor = (
            product(high[:depth], low_ref[:depth, panel])
            + product(low[:depth], high_ref[:depth, panel])
            + product(high[:depth], high_ref[:depth, panel])
        )
        out_ref[p] = jnp.where(column >= p * PANEL, factor, 0.0)


def panel_factors(strip, high, low, first):
    columns = strip.shape[1]
    wide = min(columns, 512)
    return pl.pallas_call(
        factor_kernel,
        out_shape=jax.ShapeDtypeStruct((PANELS, columns, PANEL), jnp.float32),
        grid=(columns // wide,),
        in_specs=[
            pl.BlockSpec(memory_space=pltpu.SMEM),
            pl.BlockSpec((LEAD, wide), lambda j: (0, j)),
            pl.BlockSpec((LEAD, LEAD), lambda j: (0, 0)),
            pl.BlockSpec((LEAD, LEAD), lambda j: (0, 0)),
        ],
        out_specs=pl.BlockSpec((PANELS, wide, PANEL), lambda j: (0, j, 0)),
        compiler_params=pltpu.CompilerParams(vmem_limit_bytes=48 * 1024 * 1024),
        cost_estimate=pl.CostEstimate(
            flops=10 * 10**9 * columns // 2048, bytes_accessed=columns * 8192, transcendentals=0
        ),
        name="panel_factors",
    )(first.reshape(1), strip, high, low)


def project(rows, basis, live):
    arcs, _, capacity = basis.shape
    blocks = rows.reshape(rows.shape[0], arcs, capacity, rows.shape[2])
    loadings = jnp.einsum(
        "alc,tacw->talw", basis, blocks, preferred_element_type=jnp.float32
    ).astype(jnp.bfloat16)
    cleaned = blocks.astype(jnp.float32) - jnp.einsum(
        "alc,talw->tacw", basis, loadings, preferred_element_type=jnp.float32
    )
    cleaned = jnp.where(live[None, :, :, None], cleaned, 0.0)
    return cleaned.astype(jnp.bfloat16).reshape(rows.shape)


def contract_rows(left_rows, right_rows):
    return lax.dot_general(
        left_rows, right_rows, (((0,), (0,)), ((), ())), preferred_element_type=jnp.float32
    )


def per_device(design, local_design, lengths, regularizer):
    row_count, col_width = design.shape
    tile = regularizer.shape[0]
    arc_total = lax.axis_size("arc")
    trow_total = lax.axis_size("trow")
    tcol_total = lax.axis_size("tcol")
    arc = lax.axis_index("arc")
    trow = lax.axis_index("trow")
    tcol = lax.axis_index("tcol")
    arcs_per_col = arc_total // tcol_total
    capacity = row_count // lengths.shape[0]

    live = jnp.arange(capacity, dtype=jnp.int32)[None, :] < lengths[:, None]

    basis = local_basis(local_design, lengths)
    own = project(design[None], basis, live)[0]
    piece = jnp.stack(
        [
            lax.dynamic_slice_in_dim(own, (e * trow_total + trow) * tile, tile, 1)
            for e in range(arcs_per_col)
        ]
    )

    row_ids = jnp.arange(tile, dtype=jnp.int32)
    col_ids = tcol * col_width + jnp.arange(col_width, dtype=jnp.int32)

    def tile_rows(a):
        return (jnp.asarray(a)[..., None] * trow_total + trow) * tile + row_ids

    lead_rows = trow * tile + row_ids
    lead_reg = jnp.where(arc == 0, regularizer, 0.0)

    lead_cols = jnp.arange(LEAD, dtype=jnp.int32)
    pivot_part = contract_rows(
        lax.dynamic_slice_in_dim(own, trow * tile, tile, 1), own[:, :LEAD]
    ) + jnp.where(lead_rows[:, None] == lead_cols[None, :], lead_reg[:, None], 0.0)

    lead_diagonal = jnp.where(
        (row_ids[:, None] == row_ids[None, :]) & (tcol == 0), lead_reg[:, None], 0.0
    )
    pivot, plane, both, cross = gather(
        own, piece, pivot_part, lead_diagonal, arc_total, trow_total, tcol_total
    )
    both = both.reshape(2 * row_count, col_width)
    cross = cross.reshape(tcol_total, 2 * row_count, tile)

    group = jnp.arange(tcol_total, dtype=jnp.int32)
    square = (col_ids[None, None, :] == tile_rows(2 * group + arc % 2)[:, :, None])
    tiles = jnp.where(
        square, 0.0, jnp.einsum("ynw,nv->ywv", cross, both, preferred_element_type=jnp.float32)
    ).astype(jnp.bfloat16)
    diagonals = jnp.sum(jnp.square(cross.astype(jnp.float32)), axis=1)[:, None, :]
    inverse, strip, received, diagonals_in, row_strip = lead(
        pivot, plane, tiles, diagonals, tcol_total
    )
    strip = strip.reshape(LEAD, col_width)
    row_strip = row_strip.reshape(LEAD, tile)
    normal = contract_rows(lax.dynamic_index_in_dim(cross, arc // 2, 0, False), both)
    normal = normal + jnp.sum(received.astype(jnp.float32), axis=0)
    rows_global = tile_rows(arc)
    diagonal = regularizer + jnp.sum(diagonals_in, axis=0)[0]
    normal = normal + jnp.where(rows_global[:, None] == col_ids[None, :], diagonal[:, None], 0.0)
    turned = inverse.T
    high = lax.reduce_precision(turned, exponent_bits=8, mantissa_bits=7)
    low = (turned - high).astype(jnp.bfloat16)
    high = high.astype(jnp.bfloat16)
    col_factors = panel_factors(strip, high, low, tcol * col_width)
    row_factors = panel_factors(row_strip, high, low, (arc * trow_total + trow) * tile)
    normal = normal - sum(
        lax.dot_general(
            row_factors[p],
            col_factors[p],
            (((1,), (1,)), ((), ())),
            precision=lax.Precision.HIGH,
            preferred_element_type=jnp.float32,
        )
        for p in range(PANELS)
    )
    return normal, col_factors


def solution(mesh):
    return jax.shard_map(
        per_device,
        mesh=mesh,
        in_specs=(P("arc", "tcol"), P("arc", None), P("arc"), P(("arc", "trow"))),
        out_specs=(P(("arc", "trow"), "tcol"), P(None, "tcol", None)),
        check_vma=False,
    )
```

```python
import jax
import jax.numpy as jnp
from jax import lax
from jax.experimental import pallas as pl
from jax.experimental.pallas import tpu as pltpu
from jax.sharding import PartitionSpec as P

PANEL = 512
PANELS = 2
LEAD = PANEL * PANELS
RIDGE = 0.1
BLOCK = 128
HIGHEST = lax.Precision.HIGHEST
AXES = ("arc", "trow", "tcol")


def spread(value):
    return jnp.broadcast_to(value, (8, 128))


def small_inverse(pivot):
    d = [list(row) for row in pivot]
    low = [[None] * 8 for _ in range(8)]
    root = [None] * 8
    for k in range(8):
        root[k] = lax.rsqrt(d[k][k])
        for i in range(k + 1, 8):
            low[i][k] = d[i][k] * root[k]
        for j in range(k + 1, 8):
            for i in range(j, 8):
                d[i][j] = d[i][j] - low[i][k] * low[j][k]
    inv = [[None] * 8 for _ in range(8)]
    for k in range(8):
        inv[k][k] = root[k]
        for i in range(k + 1, 8):
            acc = low[i][k] * inv[k][k]
            for m in range(k + 1, i):
                acc = acc + low[i][m] * inv[m][k]
            inv[i][k] = -acc * root[i]
    return inv


def inverse_factors(matrices):
    lane = lax.broadcasted_iota(jnp.int32, (8, 128), 1)
    sub = lax.broadcasted_iota(jnp.int32, (8, 128), 0)
    zero = jnp.zeros((8, 128), jnp.float32)
    work = [[m[8 * i : 8 * i + 8, :] for i in range(16)] for m in matrices]
    unit = [
        [jnp.where(lane == sub + 8 * i, 1.0, 0.0).astype(jnp.float32) for i in range(16)]
        for _ in matrices
    ]
    for t in range(16):
        for A, X in zip(work, unit):
            lead = 8 * t
            cols = [spread(A[t][:, lead + k : lead + k + 1]) for k in range(8)]
            pivot = [
                [spread(cols[k][i : i + 1, :]) if k <= i else None for k in range(8)]
                for i in range(8)
            ]
            inv = small_inverse(pivot)
            U, UX = zero, zero
            for k in range(8):
                c = zero
                for i in range(k, 8):
                    c = jnp.where(sub == i, inv[i][k], c)
                U = U + c * spread(A[t][k : k + 1, :])
                UX = UX + c * spread(X[t][k : k + 1, :])
            X[t] = UX
            if t == 15:
                continue
            V, VX = zero, zero
            for m in range(8):
                c = zero
                for k in range(m + 1):
                    c = jnp.where(sub == k, inv[m][k], c)
                V = V + c * spread(U[m : m + 1, :])
                VX = VX + c * spread(UX[m : m + 1, :])
            rows = [spread(V[k : k + 1, :]) for k in range(8)]
            rows_x = [spread(VX[k : k + 1, :]) for k in range(8)]
            for i in range(t + 1, 16):
                cs = [spread(A[i][:, lead + k : lead + k + 1]) for k in range(8)]
                for k in range(8):
                    A[i] = A[i] - cs[k] * rows[k]
                    X[i] = X[i] - cs[k] * rows_x[k]
    return [jnp.concatenate(X, 0) for X in unit]


def basis_kernel(lengths_ref, local_ref, basis_ref):
    arcs = basis_ref.shape[0]
    capacity = basis_ref.shape[2]
    row = lax.broadcasted_iota(jnp.int32, (capacity, BLOCK), 0)
    eye = (
        lax.broadcasted_iota(jnp.int32, (BLOCK, BLOCK), 0)
        == lax.broadcasted_iota(jnp.int32, (BLOCK, BLOCK), 1)
    )
    masked, normals = [], []
    for a in range(arcs):
        block = local_ref[a * capacity : (a + 1) * capacity, :].astype(jnp.float32)
        block = jnp.where(row < lengths_ref[a], block, 0.0)
        half = block.astype(jnp.bfloat16)
        normal = lax.dot_general(
            half, half, (((0,), (0,)), ((), ())), preferred_element_type=jnp.float32
        )
        masked.append(block)
        normals.append(normal + jnp.where(eye, RIDGE, 0.0))
    for a, inverse in enumerate(inverse_factors(normals)):
        basis = lax.dot_general(
            inverse,
            masked[a],
            (((1,), (1,)), ((), ())),
            precision=HIGHEST,
            preferred_element_type=jnp.float32,
        )
        basis_ref[a] = basis.astype(jnp.bfloat16)


def local_basis(local_design, lengths):
    arcs = lengths.shape[0]
    capacity = local_design.shape[0] // arcs
    return pl.pallas_call(
        basis_kernel,
        out_shape=jax.ShapeDtypeStruct((arcs, BLOCK, capacity), jnp.bfloat16),
        in_specs=[
            pl.BlockSpec(memory_space=pltpu.SMEM),
            pl.BlockSpec(memory_space=pltpu.VMEM),
        ],
        out_specs=pl.BlockSpec(memory_space=pltpu.VMEM),
        compiler_params=pltpu.CompilerParams(vmem_limit_bytes=32 * 1024 * 1024),
        cost_estimate=pl.CostEstimate(flops=10**9, bytes_accessed=30_000_000, transcendentals=0),
        name="local_basis",
    )(lengths, local_design)


def mesh_copy(src, dst, send, recv, device):
    return pltpu.make_async_remote_copy(
        src_ref=src,
        dst_ref=dst,
        send_sem=send,
        recv_sem=recv,
        device_id=device,
        device_id_type=pl.DeviceIdType.MESH,
    )


def greet(devices):
    barrier = pltpu.get_barrier_semaphore()
    for device in devices:
        pl.semaphore_signal(
            barrier, inc=1, device_id=device, device_id_type=pl.DeviceIdType.MESH
        )
    pl.semaphore_wait(barrier, len(devices))


def eliminate(out_ref, before):
    size = out_ref.shape[0]
    blocks = size // BLOCK
    col = lax.broadcasted_iota(jnp.int32, (BLOCK, size), 1)

    def step(k, _):
        before(k)
        base = pl.multiple_of(k * BLOCK, BLOCK)
        here = pl.ds(base, BLOCK)
        after = base + BLOCK
        inverse = inverse_factors([out_ref[here, here]])[0]
        out_ref[here, here] = jnp.where(
            lax.broadcasted_iota(jnp.int32, (BLOCK, BLOCK), 0)
            == lax.broadcasted_iota(jnp.int32, (BLOCK, BLOCK), 1),
            1.0,
            0.0,
        )
        lead_row = jnp.dot(
            inverse, out_ref[here, :], precision=HIGHEST, preferred_element_type=jnp.float32
        )
        coef = jnp.where(col >= after, lead_row, 0.0)

        def trail(first):
            below = slice(first, size)
            row = lax.broadcasted_iota(jnp.int32, (size - first, BLOCK), 0) + first
            out_ref[below, here] = jnp.where(row >= after, 0.0, out_ref[below, here])
            out_ref[below, :] = out_ref[below, :] - lax.dot_general(
                coef[:, below],
                lead_row,
                (((0,), (0,)), ((), ())),
                precision=HIGHEST,
                preferred_element_type=jnp.float32,
            )

        half = blocks // 2

        @pl.when(k < half)
        def _():
            trail(BLOCK)

        @pl.when((k >= half) & (k < blocks - 1))
        def _():
            trail((half + 1) * BLOCK)

        out_ref[here, :] = jnp.where(col < after, lead_row, 0.0)
        return 0

    lax.fori_loop(0, blocks, step, 0)


def gather_kernel(
    own, piece, pivot_part, regs, pivot, strip_out, both, cross,
    pivot_in, strip_part, strip_in, chunk, half, stack, total_ref, first, swap_in, pair_sum, pair_in,
    first_send, first_recv, swap_send, swap_recv, mine_send, mine_recv,
    theirs_send, theirs_recv, plane_send, plane_recv,
    part_send, part_recv, half_send, half_recv, stack_send, stack_recv,
    lead_send, lead_recv, core_send, core_recv, strip_send, strip_recv,
    wide_send, wide_recv, relay_send, relay_recv, pair_send, pair_recv, own_sem, local_sem,
):
    trows, arcs, cores, depth, width = pivot.shape
    share = total_ref.shape[0]
    tcols = half_send.shape[0]
    tile = width // trows
    a, r, c = lax.axis_index("arc"), lax.axis_index("trow"), lax.axis_index("tcol")
    core = lax.rem(c, 2)
    parity = lax.rem(a, 2)
    others = range(1, arcs)
    greet(
        [(a ^ m, r, c) for m in others]
        + [(a, r ^ q, c) for q in range(1, trows)]
        + [(a, r, c ^ q) for q in range(1, tcols)]
    )

    def rows_of(part, target):
        return part.at[pl.ds(pl.multiple_of(target * share, share), share)]

    parts = [
        mesh_copy(
            rows_of(pivot_part, a ^ m), pivot_in.at[m],
            part_send.at[m], part_recv.at[m], (a ^ m, r, c),
        )
        for m in others
    ]
    groups = arcs // 2
    beyond = range(1, groups)
    strips = [
        mesh_copy(
            strip_part.at[pl.ds(pl.multiple_of((a // 2 ^ m) * 2 * share, 2 * share), 2 * share)],
            strip_in.at[m],
            strip_send.at[m], strip_recv.at[m], (a ^ (2 * m), r, c),
        )
        for m in beyond
    ]
    firsts = [
        mesh_copy(piece.at[0], first, first_send.at[q], first_recv, (a, r, q))
        for q in range(1, tcols)
    ]
    swap = mesh_copy(piece, swap_in, swap_send, swap_recv, (a ^ 1, r, c))
    mine = [
        mesh_copy(
            piece.at[parity], cross.at[c, 0], mine_send.at[q], mine_recv.at[q], (a, r, c ^ q)
        )
        for q in (1, 2)
    ]
    theirs = [
        mesh_copy(
            swap_in.at[parity], cross.at[c, 1], theirs_send.at[q], theirs_recv.at[q], (a, r, c ^ q)
        )
        for q in (1, 2)
    ]
    relays = [
        mesh_copy(
            cross.at[c ^ 2], cross.at[c ^ 2], relay_send.at[0], relay_recv.at[0], (a, r, c ^ 1)
        )
    ]

    def spot(e):
        return pl.ds(pl.multiple_of((e * trows + r) * tile, tile), tile)

    planes = [
        mesh_copy(
            swap_in.at[e], both.at[1, :, spot(e)],
            plane_send.at[q, e], plane_recv.at[q, e], (a, r ^ q, c),
        )
        for q in range(1, trows)
        for e in range(piece.shape[0])
    ]

    @pl.when(c == 0)
    def _():
        for copy in parts + firsts:
            copy.start()
        first[...] = piece[0]

    swap.start()
    keep_mine = pltpu.make_async_copy(piece.at[parity], cross.at[c, 0], local_sem.at[0])
    keep_mine.start()
    keep_own = pltpu.make_async_copy(own, both.at[0], local_sem.at[4])
    keep_own.start()
    for copy in mine:
        copy.start()

    @pl.when(c != 0)
    def _():
        mesh_copy(piece.at[0], first, first_send.at[0], first_recv, (a, r, c ^ 1)).wait_recv()

    wide = 512
    for j in range(0, own.shape[1], wide):
        strip_part[:, j : j + wide] = lax.dot_general(
            first[...],
            own[:, j : j + wide],
            (((0,), (0,)), ((), ())),
            preferred_element_type=jnp.float32,
        )
    lead = pl.ds(pl.multiple_of(r * tile, tile), tile)
    strip_part[:, lead] = strip_part[:, lead] + regs[...]
    for copy in strips:
        copy.start()

    @pl.when(c == 0)
    def _():
        total = rows_of(pivot_part, a)[...]
        for m, copy in enumerate(parts):
            copy.wait_recv()
            total = total + pivot_in[m + 1]
        chunk[...] = total.reshape(chunk.shape)
        spreads = [
            mesh_copy(chunk.at[q % 2], half, half_send.at[q], half_recv, (a, r, q))
            for q in range(1, tcols)
        ]
        for copy in spreads:
            copy.start()
        half[...] = chunk[0]
        for copy in parts + firsts + spreads:
            copy.wait_send()

    @pl.when(c != 0)
    def _():
        mesh_copy(chunk.at[0], half, half_send.at[0], half_recv, (a, r, c ^ 1)).wait_recv()

    stacked = [
        mesh_copy(half, stack.at[r], stack_send.at[q], stack_recv.at[q], (a, r ^ q, c))
        for q in range(1, trows)
    ]
    for copy in stacked:
        copy.start()
    stack[r] = half[...]
    swap.wait_recv()
    for copy in theirs + planes:
        copy.start()
    keep_theirs = pltpu.make_async_copy(swap_in.at[parity], cross.at[c, 1], local_sem.at[1])
    keep_planes = [
        pltpu.make_async_copy(swap_in.at[e], both.at[1, :, spot(e)], local_sem.at[2 + e])
        for e in range(piece.shape[0])
    ]
    for copy in [keep_theirs] + keep_planes:
        copy.start()
    for copy in stacked:
        copy.wait_recv()

    def columns(t):
        return pl.ds(t * tile, width - t * tile)

    leads = [
        [
            mesh_copy(
                stack.at[t, :, columns(t)], pivot.at[t, a, core, :, columns(t)],
                lead_send.at[m, t], lead_recv.at[m, t], (a ^ m, r, c),
            )
            for m in others
        ]
        for t in range(trows)
    ]
    for group in leads:
        for copy in group:
            copy.start()
    for t in range(trows):
        pivot[t, a, core] = stack[t]

    total = strip_part[pl.ds(pl.multiple_of(a // 2 * 2 * share, 2 * share), 2 * share)]
    for m, copy in enumerate(strips):
        copy.wait_recv()
        total = total + strip_in[m + 1]
    pair_sum[...] = total
    pair = mesh_copy(
        rows_of(pair_sum, 1 - parity), pair_in, pair_send, pair_recv, (a ^ 1, r, c)
    )
    pair.start()
    for copy in mine + theirs:
        copy.wait_recv()
    for copy in relays:
        copy.start()
    pair.wait_recv()
    total_ref[...] = rows_of(pair_sum, parity)[...] + pair_in[...]
    own_copy = pltpu.make_async_copy(total_ref, strip_out.at[a], own_sem)
    own_copy.start()
    wides = [
        mesh_copy(total_ref, strip_out.at[a], wide_send.at[m], wide_recv.at[m], (a ^ m, r, c))
        for m in [1] + [2 * m for m in beyond]
    ]
    for copy in wides:
        copy.start()
    wides[0].wait_recv()
    onward = [
        mesh_copy(
            strip_out.at[a ^ 1], strip_out.at[a ^ 1],
            relay_send.at[m], relay_recv.at[m], (a ^ (2 * m), r, c),
        )
        for m in beyond
    ]
    for copy in onward:
        copy.start()

    swaps = []
    for t in range(trows):
        for copy in leads[t]:
            copy.wait_recv()
        copy = mesh_copy(
            pivot.at[t, :, core, :, columns(t)], pivot.at[t, :, core, :, columns(t)],
            core_send.at[t], core_recv.at[t], (a, r, c ^ 1),
        )
        copy.start()
        swaps.append(copy)
    for copy in swaps + planes + relays + wides[1:] + onward:
        copy.wait()
    for copy in [keep_own, keep_mine, keep_theirs, own_copy] + keep_planes:
        copy.wait()
    sent = [swap, pair, wides[0]] + mine + theirs + stacked + strips
    for copy in sent + [copy for group in leads for copy in group]:
        copy.wait_send()


def gather(own, piece, pivot_part, regs, arcs, trows, tcols):
    tile, width = pivot_part.shape
    rows, columns = own.shape
    share = tile // arcs
    depth = share // 2
    dma = pltpu.SemaphoreType.DMA
    vmem = pl.BlockSpec(memory_space=pltpu.VMEM)
    anywhere = pl.BlockSpec(memory_space=pl.ANY)
    return pl.pallas_call(
        gather_kernel,
        out_shape=(
            jax.ShapeDtypeStruct((trows, arcs, 2, depth, width), jnp.float32),
            jax.ShapeDtypeStruct((arcs, share, columns), jnp.float32),
            jax.ShapeDtypeStruct((2,) + own.shape, own.dtype),
            jax.ShapeDtypeStruct((tcols, 2) + piece.shape[1:], piece.dtype),
        ),
        in_specs=[vmem] * 4,
        out_specs=(vmem, anywhere, anywhere, anywhere),
        scratch_shapes=[
            pltpu.VMEM((arcs, share, width), jnp.float32),
            pltpu.VMEM((tile, columns), jnp.float32),
            pltpu.VMEM((arcs // 2, 2 * share, columns), jnp.float32),
            pltpu.VMEM((2, depth, width), jnp.float32),
            pltpu.VMEM((depth, width), jnp.float32),
            pltpu.VMEM((trows, depth, width), jnp.float32),
            pltpu.VMEM((share, columns), jnp.float32),
            pltpu.VMEM(piece.shape[1:], piece.dtype),
            pltpu.VMEM(piece.shape, piece.dtype),
            pltpu.VMEM((2 * share, columns), jnp.float32),
            pltpu.VMEM((share, columns), jnp.float32),
            dma((tcols,)), dma,
            dma, dma,
            dma((tcols,)), dma((tcols,)),
            dma((tcols,)), dma((tcols,)),
            dma((trows, 2)), dma((trows, 2)),
            dma((arcs,)), dma((arcs,)),
            dma((tcols,)), dma,
            dma((trows,)), dma((trows,)),
            dma((arcs, trows)), dma((arcs, trows)),
            dma((trows,)), dma((trows,)),
            dma((arcs,)), dma((arcs,)),
            dma((arcs,)), dma((arcs,)),
            dma((arcs // 2,)), dma((arcs // 2,)),
            dma, dma,
            dma, dma((5,)),
        ],
        compiler_params=pltpu.CompilerParams(
            collective_id=0, has_side_effects=True, vmem_limit_bytes=40 * 1024 * 1024
        ),
        cost_estimate=pl.CostEstimate(
            flops=40 * 10**9, bytes_accessed=250_000_000, transcendentals=0
        ),
        name="gather",
    )(own, piece, pivot_part, regs)


def lead_kernel(
    pivot, plane, cross, both, diagonals, regs, high_ref, low_ref, strip_out, rows_out, normal,
    inverse_ref, tiles, received, diagonals_in,
    near_send, near_recv, far_send, far_recv, tile_send, tile_recv, own_sem,
    diagonal_send, diagonal_recv, row_send, row_recv, row_local,
):
    trows, arcs = strip_out.shape[:2]
    groups = cross.shape[0]
    a, r, c = lax.axis_index("arc"), lax.axis_index("trow"), lax.axis_index("tcol")
    up, down = lax.rem(r + 1, trows), lax.rem(r + trows - 1, trows)
    group = a // 2
    tcols = row_send.shape[1]
    tile = rows_out.shape[-1]
    greet(
        [(a ^ (2 * m), r, c) for m in range(1, groups)]
        + [(a, up, c), (a, down, c)]
        + [(a, r, c ^ q) for q in range(1, tcols)]
    )
    some = arcs // 2
    near = [
        mesh_copy(plane, strip_out.at[r], near_send.at[i], near_recv.at[i], (a, z, c))
        for i, z in enumerate((up, down))
    ]
    far = [
        mesh_copy(
            strip_out.at[z, part], strip_out.at[z, part],
            far_send.at[i], far_recv.at[i], (a, to, c),
        )
        for i, (z, part, to) in enumerate(
            ((down, pl.ds(0, some), up), (up, pl.ds(some, some), down))
        )
    ]
    exchanges = [
        mesh_copy(
            tiles.at[group ^ m], received.at[m - 1],
            tile_send.at[m - 1], tile_recv.at[m - 1], (a ^ (2 * m), r, c),
        )
        for m in range(1, groups)
    ]
    corners = [
        mesh_copy(
            diagonals.at[group ^ m], diagonals_in.at[m - 1],
            diagonal_send.at[m - 1], diagonal_recv.at[m - 1], (a ^ (2 * m), r, c),
        )
        for m in range(1, groups)
    ]

    holder = c == group
    spot = pl.ds(pl.multiple_of((lax.rem(a, 2) * trows + r) * tile, tile), tile)
    places = (r, up, down, lax.rem(r + 2, trows))

    def row_copies(i):
        source = (plane if i == 0 else strip_out.at[places[i]]).at[:, :, spot]
        target = rows_out.at[places[i]]
        away = [
            mesh_copy(source, target, row_send.at[i, q], row_recv.at[i], (a, r, c ^ q))
            for q in range(1, tcols)
        ]
        return away, pltpu.make_async_copy(source, target, row_local.at[i])

    def send_rows(i):
        @pl.when(holder)
        def _():
            away, here = row_copies(i)
            for copy in away:
                copy.start()
            here.start()

    for copy in near + corners:
        copy.start()
    send_rows(0)
    keep = pltpu.make_async_copy(plane, strip_out.at[r], own_sem)
    keep.start()

    def product(g):
        return lax.dot_general(
            cross[g], both[...], (((0,), (0,)), ((), ())), preferred_element_type=jnp.float32
        )

    eye = (
        lax.broadcasted_iota(jnp.int32, (tile, tile), 0)
        == lax.broadcasted_iota(jnp.int32, (tile, tile), 1)
    )

    def send_tile(i, _):
        g = group ^ (i + 1)
        tiles[g] = product(g).astype(tiles.dtype)

        @pl.when(c == g)
        def _():
            square = jnp.where(eye, 0.0, tiles[g, :, spot].astype(jnp.float32))
            tiles[g, :, spot] = square.astype(tiles.dtype)

        mesh_copy(
            tiles.at[g], received.at[i], tile_send.at[i], tile_recv.at[i], (a ^ (2 * (i + 1)), r, c)
        ).start()
        return 0

    lax.fori_loop(0, groups - 1, send_tile, 0)
    inverse_ref[...] = pivot[...].reshape(inverse_ref.shape)

    def before(k):
        @pl.when(k == 5)
        def _():
            for copy in near:
                copy.wait_recv()
            for copy in far:
                copy.start()
            send_rows(1)
            send_rows(2)

    eliminate(inverse_ref, before)
    for copy in far:
        copy.wait_recv()
    send_rows(3)

    def turn(i, _):
        here = pl.ds(pl.multiple_of(i * BLOCK, BLOCK), BLOCK)
        high_ref[:, here], low_ref[:, here] = halves(inverse_ref[here, :].T)
        return 0

    lax.fori_loop(0, inverse_ref.shape[0] // BLOCK, turn, 0)
    normal[...] = product(group)
    for copy in exchanges + corners:
        copy.wait()
    diagonal = regs[...]
    for i in range(groups - 1):
        normal[...] = normal[...] + received[i].astype(jnp.float32)
        diagonal = diagonal + diagonals_in[i]

    @pl.when(holder)
    def _():
        normal[:, spot] = normal[:, spot] + jnp.where(eye, diagonal, 0.0)

    @pl.when(holder)
    def _():
        for i in range(len(places)):
            away, here = row_copies(i)
            for copy in away:
                copy.wait_send()
            here.wait()

    @pl.when(jnp.logical_not(holder))
    def _():
        for i in range(len(places)):
            row_copies(i)[0][0].wait_recv()

    for copy in far:
        copy.wait_send()
    for copy in near:
        copy.wait_send()
    keep.wait()


def lead(pivot, plane, cross, both, diagonals, regs):
    trows, arcs = pivot.shape[:2]
    width = pivot.shape[-1]
    groups, _, tile = cross.shape
    columns = both.shape[1]
    half = both.dtype
    dma = pltpu.SemaphoreType.DMA
    vmem = pl.BlockSpec(memory_space=pltpu.VMEM)
    anywhere = pl.BlockSpec(memory_space=pl.ANY)
    return pl.pallas_call(
        lead_kernel,
        out_shape=(
            jax.ShapeDtypeStruct((width, width), half),
            jax.ShapeDtypeStruct((width, width), half),
            jax.ShapeDtypeStruct((trows,) + plane.shape, jnp.float32),
            jax.ShapeDtypeStruct((trows,) + plane.shape[:2] + (tile,), jnp.float32),
            jax.ShapeDtypeStruct((tile, columns), jnp.float32),
        ),
        in_specs=[vmem, anywhere, vmem, vmem, vmem, vmem],
        out_specs=(vmem, vmem, anywhere, anywhere, vmem),
        scratch_shapes=[
            pltpu.VMEM((width, width), jnp.float32),
            pltpu.VMEM((groups, tile, columns), half),
            pltpu.VMEM((groups - 1, tile, columns), half),
            pltpu.VMEM((groups - 1, 1, tile), jnp.float32),
            dma((2,)), dma((2,)),
            dma((2,)), dma((2,)),
            dma((groups - 1,)), dma((groups - 1,)),
            dma,
            dma((groups - 1,)), dma((groups - 1,)),
            dma((trows, groups)), dma((trows,)), dma((trows,)),
        ],
        compiler_params=pltpu.CompilerParams(
            collective_id=1, has_side_effects=True, vmem_limit_bytes=52 * 1024 * 1024
        ),
        cost_estimate=pl.CostEstimate(
            flops=80 * 10**9, bytes_accessed=250_000_000, transcendentals=0
        ),
        name="lead",
    )(pivot, plane, cross, both, diagonals, regs)


def halves(value):
    high = value.astype(jnp.bfloat16)
    return high, (value - high.astype(jnp.float32)).astype(jnp.bfloat16)


def products(left, right, dims):
    def one(x, y):
        return lax.dot_general(x, y, (dims, ((), ())), preferred_element_type=jnp.float32)

    return one(left[0], right[1]) + one(left[1], right[0]) + one(left[0], right[0])


def finish_kernel(
    first_ref, strip_ref, high_ref, low_ref, rows_ref, normal_ref, factor_out, normal_out,
    row_high, row_low,
):
    def factors(columns, first):
        high, low = halves(columns)
        ids = first + lax.broadcasted_iota(jnp.int32, (columns.shape[1], PANEL), 0)
        for p in range(PANELS):
            depth = (p + 1) * PANEL
            panel = slice(p * PANEL, depth)
            factor = products(
                (high[:depth], low[:depth]),
                (high_ref[:depth, panel], low_ref[:depth, panel]),
                ((0,), (0,)),
            )
            yield jnp.where(ids >= p * PANEL, factor, 0.0)

    @pl.when(pl.program_id(0) == 0)
    def _():
        for p, factor in enumerate(factors(rows_ref[...], first_ref[1])):
            row_high[p], row_low[p] = halves(factor)

    total = normal_ref[...]
    wide = strip_ref.shape[1]
    for p, factor in enumerate(factors(strip_ref[...], first_ref[0] + pl.program_id(0) * wide)):
        factor_out[p] = factor
        total = total - products((row_high[p], row_low[p]), halves(factor), ((1,), (1,)))
    normal_out[...] = total


def finish(strip, high, low, rows, normal, first):
    columns = strip.shape[1]
    tile = normal.shape[0]
    wide = 512
    return pl.pallas_call(
        finish_kernel,
        out_shape=(
            jax.ShapeDtypeStruct((PANELS, columns, PANEL), jnp.float32),
            jax.ShapeDtypeStruct(normal.shape, jnp.float32),
        ),
        grid=(columns // wide,),
        in_specs=[
            pl.BlockSpec(memory_space=pltpu.SMEM),
            pl.BlockSpec((LEAD, wide), lambda j: (0, j)),
            pl.BlockSpec((LEAD, LEAD), lambda j: (0, 0)),
            pl.BlockSpec((LEAD, LEAD), lambda j: (0, 0)),
            pl.BlockSpec((LEAD, tile), lambda j: (0, 0)),
            pl.BlockSpec((tile, wide), lambda j: (0, j)),
        ],
        out_specs=(
            pl.BlockSpec((PANELS, wide, PANEL), lambda j: (0, j, 0)),
            pl.BlockSpec((tile, wide), lambda j: (0, j)),
        ),
        scratch_shapes=[
            pltpu.VMEM((PANELS, tile, PANEL), jnp.bfloat16),
            pltpu.VMEM((PANELS, tile, PANEL), jnp.bfloat16),
        ],
        compiler_params=pltpu.CompilerParams(vmem_limit_bytes=52 * 1024 * 1024),
        cost_estimate=pl.CostEstimate(
            flops=14 * 10**9, bytes_accessed=25_000_000, transcendentals=0
        ),
        name="finish",
    )(first, strip, high, low, rows, normal)


def project(rows, basis, live):
    arcs, _, capacity = basis.shape
    blocks = rows.reshape(rows.shape[0], arcs, capacity, rows.shape[2])
    loadings = jnp.einsum(
        "alc,tacw->talw", basis, blocks, preferred_element_type=jnp.float32
    ).astype(jnp.bfloat16)
    cleaned = blocks.astype(jnp.float32) - jnp.einsum(
        "alc,talw->tacw", basis, loadings, preferred_element_type=jnp.float32
    )
    cleaned = jnp.where(live[None, :, :, None], cleaned, 0.0)
    return cleaned.astype(jnp.bfloat16).reshape(rows.shape)


def contract_rows(left_rows, right_rows):
    return lax.dot_general(
        left_rows, right_rows, (((0,), (0,)), ((), ())), preferred_element_type=jnp.float32
    )


def per_device(design, local_design, lengths, regularizer):
    row_count, col_width = design.shape
    tile = regularizer.shape[0]
    arc_total = lax.axis_size("arc")
    trow_total = lax.axis_size("trow")
    tcol_total = lax.axis_size("tcol")
    arc = lax.axis_index("arc")
    trow = lax.axis_index("trow")
    tcol = lax.axis_index("tcol")
    arcs_per_col = arc_total // tcol_total
    capacity = row_count // lengths.shape[0]

    live = jnp.arange(capacity, dtype=jnp.int32)[None, :] < lengths[:, None]

    basis = local_basis(local_design, lengths)
    own = project(design[None], basis, live)[0]
    piece = jnp.stack(
        [
            lax.dynamic_slice_in_dim(own, (e * trow_total + trow) * tile, tile, 1)
            for e in range(arcs_per_col)
        ]
    )

    row_ids = jnp.arange(tile, dtype=jnp.int32)
    lead_rows = trow * tile + row_ids
    lead_reg = jnp.where(arc == 0, regularizer, 0.0)

    lead_cols = jnp.arange(LEAD, dtype=jnp.int32)
    pivot_part = contract_rows(
        lax.dynamic_slice_in_dim(own, trow * tile, tile, 1), own[:, :LEAD]
    ) + jnp.where(lead_rows[:, None] == lead_cols[None, :], lead_reg[:, None], 0.0)

    lead_diagonal = jnp.where(
        (row_ids[:, None] == row_ids[None, :]) & (tcol == 0), lead_reg[:, None], 0.0
    )
    pivot, plane, both, cross = gather(
        own, piece, pivot_part, lead_diagonal, arc_total, trow_total, tcol_total
    )
    both = both.reshape(2 * row_count, col_width)
    cross = cross.reshape(tcol_total, 2 * row_count, tile)

    diagonals = jnp.sum(jnp.square(cross.astype(jnp.float32)), axis=1)[:, None, :]
    high, low, strip, row_strip, normal = lead(
        pivot, plane, cross, both, diagonals, regularizer[None, :]
    )
    first = jnp.stack([tcol * col_width, (arc * trow_total + trow) * tile])
    factors, normal = finish(
        strip.reshape(LEAD, col_width), high, low, row_strip.reshape(LEAD, tile), normal, first
    )
    return normal, factors


def solution(mesh):
    return jax.shard_map(
        per_device,
        mesh=mesh,
        in_specs=(P("arc", "tcol"), P("arc", None), P("arc"), P(("arc", "trow"))),
        out_specs=(P(("arc", "trow"), "tcol"), P(None, "tcol", None)),
        check_vma=False,
    )
```

```python
import jax
import jax.numpy as jnp
from jax import lax
from jax.experimental import pallas as pl
from jax.experimental.pallas import tpu as pltpu
from jax.sharding import PartitionSpec as P

PANEL = 512
PANELS = 2
LEAD = PANEL * PANELS
RIDGE = 0.1
BLOCK = 128
HIGHEST = lax.Precision.HIGHEST
AXES = ("arc", "trow", "tcol")


def spread(value):
    return jnp.broadcast_to(value, (8, 128))


def small_inverse(pivot):
    d = [list(row) for row in pivot]
    low = [[None] * 8 for _ in range(8)]
    root = [None] * 8
    for k in range(8):
        root[k] = lax.rsqrt(d[k][k])
        for i in range(k + 1, 8):
            low[i][k] = d[i][k] * root[k]
        for j in range(k + 1, 8):
            for i in range(j, 8):
                d[i][j] = d[i][j] - low[i][k] * low[j][k]
    inv = [[None] * 8 for _ in range(8)]
    for k in range(8):
        inv[k][k] = root[k]
        for i in range(k + 1, 8):
            acc = low[i][k] * inv[k][k]
            for m in range(k + 1, i):
                acc = acc + low[i][m] * inv[m][k]
            inv[i][k] = -acc * root[i]
    return inv


def inverse_factors(matrices):
    lane = lax.broadcasted_iota(jnp.int32, (8, 128), 1)
    sub = lax.broadcasted_iota(jnp.int32, (8, 128), 0)
    zero = jnp.zeros((8, 128), jnp.float32)
    work = [[m[8 * i : 8 * i + 8, :] for i in range(16)] for m in matrices]
    unit = [
        [jnp.where(lane == sub + 8 * i, 1.0, 0.0).astype(jnp.float32) for i in range(16)]
        for _ in matrices
    ]
    for t in range(16):
        for A, X in zip(work, unit):
            lead = 8 * t
            cols = [spread(A[t][:, lead + k : lead + k + 1]) for k in range(8)]
            pivot = [
                [spread(cols[k][i : i + 1, :]) if k <= i else None for k in range(8)]
                for i in range(8)
            ]
            inv = small_inverse(pivot)
            U, UX = zero, zero
            for k in range(8):
                c = zero
                for i in range(k, 8):
                    c = jnp.where(sub == i, inv[i][k], c)
                U = U + c * spread(A[t][k : k + 1, :])
                UX = UX + c * spread(X[t][k : k + 1, :])
            X[t] = UX
            if t == 15:
                continue
            V, VX = zero, zero
            for m in range(8):
                c = zero
                for k in range(m + 1):
                    c = jnp.where(sub == k, inv[m][k], c)
                V = V + c * spread(U[m : m + 1, :])
                VX = VX + c * spread(UX[m : m + 1, :])
            rows = [spread(V[k : k + 1, :]) for k in range(8)]
            rows_x = [spread(VX[k : k + 1, :]) for k in range(8)]
            for i in range(t + 1, 16):
                cs = [spread(A[i][:, lead + k : lead + k + 1]) for k in range(8)]
                for k in range(8):
                    A[i] = A[i] - cs[k] * rows[k]
                    X[i] = X[i] - cs[k] * rows_x[k]
    return [jnp.concatenate(X, 0) for X in unit]


def basis_kernel(lengths_ref, local_ref, basis_ref):
    arcs = basis_ref.shape[0]
    capacity = basis_ref.shape[2]
    row = lax.broadcasted_iota(jnp.int32, (capacity, BLOCK), 0)
    eye = (
        lax.broadcasted_iota(jnp.int32, (BLOCK, BLOCK), 0)
        == lax.broadcasted_iota(jnp.int32, (BLOCK, BLOCK), 1)
    )
    masked, normals = [], []
    for a in range(arcs):
        block = local_ref[a * capacity : (a + 1) * capacity, :].astype(jnp.float32)
        block = jnp.where(row < lengths_ref[a], block, 0.0)
        half = block.astype(jnp.bfloat16)
        normal = lax.dot_general(
            half, half, (((0,), (0,)), ((), ())), preferred_element_type=jnp.float32
        )
        masked.append(block)
        normals.append(normal + jnp.where(eye, RIDGE, 0.0))
    for a, inverse in enumerate(inverse_factors(normals)):
        basis = lax.dot_general(
            inverse,
            masked[a],
            (((1,), (1,)), ((), ())),
            precision=HIGHEST,
            preferred_element_type=jnp.float32,
        )
        basis_ref[a] = basis.astype(jnp.bfloat16)


def local_basis(local_design, lengths):
    arcs = lengths.shape[0]
    capacity = local_design.shape[0] // arcs
    return pl.pallas_call(
        basis_kernel,
        out_shape=jax.ShapeDtypeStruct((arcs, BLOCK, capacity), jnp.bfloat16),
        in_specs=[
            pl.BlockSpec(memory_space=pltpu.SMEM),
            pl.BlockSpec(memory_space=pltpu.VMEM),
        ],
        out_specs=pl.BlockSpec(memory_space=pltpu.VMEM),
        compiler_params=pltpu.CompilerParams(vmem_limit_bytes=32 * 1024 * 1024),
        cost_estimate=pl.CostEstimate(flops=10**9, bytes_accessed=30_000_000, transcendentals=0),
        name="local_basis",
    )(lengths, local_design)


def mesh_copy(src, dst, send, recv, device):
    return pltpu.make_async_remote_copy(
        src_ref=src,
        dst_ref=dst,
        send_sem=send,
        recv_sem=recv,
        device_id=device,
        device_id_type=pl.DeviceIdType.MESH,
    )


def greet(devices):
    barrier = pltpu.get_barrier_semaphore()
    for device in devices:
        pl.semaphore_signal(
            barrier, inc=1, device_id=device, device_id_type=pl.DeviceIdType.MESH
        )
    pl.semaphore_wait(barrier, len(devices))


def eliminate(out_ref, before):
    size = out_ref.shape[0]
    blocks = size // BLOCK
    col = lax.broadcasted_iota(jnp.int32, (BLOCK, size), 1)

    def step(k, _):
        before(k)
        base = pl.multiple_of(k * BLOCK, BLOCK)
        here = pl.ds(base, BLOCK)
        after = base + BLOCK
        inverse = inverse_factors([out_ref[here, here]])[0]
        out_ref[here, here] = jnp.where(
            lax.broadcasted_iota(jnp.int32, (BLOCK, BLOCK), 0)
            == lax.broadcasted_iota(jnp.int32, (BLOCK, BLOCK), 1),
            1.0,
            0.0,
        )
        lead_row = jnp.dot(
            inverse, out_ref[here, :], precision=HIGHEST, preferred_element_type=jnp.float32
        )
        coef = jnp.where(col >= after, lead_row, 0.0)

        def trail(first):
            below = slice(first, size)
            row = lax.broadcasted_iota(jnp.int32, (size - first, BLOCK), 0) + first
            out_ref[below, here] = jnp.where(row >= after, 0.0, out_ref[below, here])
            out_ref[below, :] = out_ref[below, :] - lax.dot_general(
                coef[:, below],
                lead_row,
                (((0,), (0,)), ((), ())),
                precision=HIGHEST,
                preferred_element_type=jnp.float32,
            )

        half = blocks // 2

        @pl.when(k < half)
        def _():
            trail(BLOCK)

        @pl.when((k >= half) & (k < blocks - 1))
        def _():
            trail((half + 1) * BLOCK)

        out_ref[here, :] = jnp.where(col < after, lead_row, 0.0)
        return 0

    lax.fori_loop(0, blocks, step, 0)


def gather_kernel(
    own, piece, pivot_part, regs, pivot, strip_out, both, cross,
    pivot_in, strip_part, strip_in, chunk, half, stack, total_ref, first, swap_in, pair_sum, pair_in,
    first_send, first_recv, swap_send, swap_recv, mine_send, mine_recv,
    theirs_send, theirs_recv, plane_send, plane_recv,
    part_send, part_recv, half_send, half_recv, stack_send, stack_recv,
    lead_send, lead_recv, core_send, core_recv, strip_send, strip_recv,
    wide_send, wide_recv, relay_send, relay_recv, pair_send, pair_recv, own_sem, local_sem,
):
    trows, arcs, cores, depth, width = pivot.shape
    share = total_ref.shape[0]
    tcols = half_send.shape[0]
    tile = width // trows
    a, r, c = lax.axis_index("arc"), lax.axis_index("trow"), lax.axis_index("tcol")
    core = lax.rem(c, 2)
    parity = lax.rem(a, 2)
    others = range(1, arcs)
    greet(
        [(a ^ m, r, c) for m in others]
        + [(a, r ^ q, c) for q in range(1, trows)]
        + [(a, r, c ^ q) for q in range(1, tcols)]
    )

    def rows_of(part, target):
        return part.at[pl.ds(pl.multiple_of(target * share, share), share)]

    parts = [
        mesh_copy(
            rows_of(pivot_part, a ^ m), pivot_in.at[m],
            part_send.at[m], part_recv.at[m], (a ^ m, r, c),
        )
        for m in others
    ]
    groups = arcs // 2
    beyond = range(1, groups)
    strips = [
        mesh_copy(
            strip_part.at[pl.ds(pl.multiple_of((a // 2 ^ m) * 2 * share, 2 * share), 2 * share)],
            strip_in.at[m],
            strip_send.at[m], strip_recv.at[m], (a ^ (2 * m), r, c),
        )
        for m in beyond
    ]
    firsts = [
        mesh_copy(piece.at[0], first, first_send.at[q], first_recv, (a, r, q))
        for q in (1, 2)
    ]
    first_on = mesh_copy(first, first, first_send.at[3], first_recv, (a, r, c ^ 1))
    swap = mesh_copy(piece, swap_in, swap_send, swap_recv, (a ^ 1, r, c))
    mine = [
        mesh_copy(
            piece.at[parity], cross.at[c, 0], mine_send.at[q], mine_recv.at[q], (a, r, c ^ q)
        )
        for q in (1, 2)
    ]
    theirs = [
        mesh_copy(
            swap_in.at[parity], cross.at[c, 1], theirs_send.at[q], theirs_recv.at[q], (a, r, c ^ q)
        )
        for q in (1, 2)
    ]
    relays = [
        mesh_copy(
            cross.at[c ^ 2], cross.at[c ^ 2], relay_send.at[0], relay_recv.at[0], (a, r, c ^ 1)
        )
    ]

    def spot(e):
        return pl.ds(pl.multiple_of((e * trows + r) * tile, tile), tile)

    planes = [
        mesh_copy(
            swap_in.at[e], both.at[1, :, spot(e)],
            plane_send.at[q, e], plane_recv.at[q, e], (a, r ^ q, c),
        )
        for q in range(1, trows)
        for e in range(piece.shape[0])
    ]

    @pl.when(c == 0)
    def _():
        for copy in firsts + parts:
            copy.start()
        first[...] = piece[0]
        for copy in firsts:
            copy.wait_send()

    @pl.when(c != 0)
    def _():
        first_on.wait_recv()

    @pl.when(c == 2)
    def _():
        first_on.start()

    swap.start()
    keep_mine = pltpu.make_async_copy(piece.at[parity], cross.at[c, 0], local_sem.at[0])
    keep_mine.start()
    keep_own = pltpu.make_async_copy(own, both.at[0], local_sem.at[4])
    keep_own.start()

    wide = 512
    for j in range(0, own.shape[1], wide):
        strip_part[:, j : j + wide] = lax.dot_general(
            first[...],
            own[:, j : j + wide],
            (((0,), (0,)), ((), ())),
            preferred_element_type=jnp.float32,
        )
    lead = pl.ds(pl.multiple_of(r * tile, tile), tile)
    strip_part[:, lead] = strip_part[:, lead] + regs[...]
    for copy in strips:
        copy.start()

    @pl.when(c == 0)
    def _():
        total = rows_of(pivot_part, a)[...]
        for m, copy in enumerate(parts):
            copy.wait_recv()
            total = total + pivot_in[m + 1]
        chunk[...] = total.reshape(chunk.shape)
        spreads = [
            mesh_copy(chunk.at[q % 2], half, half_send.at[q], half_recv, (a, r, q))
            for q in range(1, tcols)
        ]
        for copy in spreads:
            copy.start()
        half[...] = chunk[0]
        for copy in parts + spreads:
            copy.wait_send()

    @pl.when(c != 0)
    def _():
        mesh_copy(chunk.at[0], half, half_send.at[0], half_recv, (a, r, c ^ 1)).wait_recv()

    @pl.when(c == 2)
    def _():
        first_on.wait_send()

    stacked = [
        mesh_copy(half, stack.at[a], stack_send.at[m], stack_recv.at[m], (a ^ m, r, c))
        for m in others
    ]
    for copy in stacked:
        copy.start()
    stack[a] = half[...]
    swap.wait_recv()
    for copy in planes + mine + theirs:
        copy.start()
    keep_theirs = pltpu.make_async_copy(swap_in.at[parity], cross.at[c, 1], local_sem.at[1])
    keep_planes = [
        pltpu.make_async_copy(swap_in.at[e], both.at[1, :, spot(e)], local_sem.at[2 + e])
        for e in range(piece.shape[0])
    ]
    for copy in [keep_theirs] + keep_planes:
        copy.start()
    for copy in stacked:
        copy.wait_recv()

    def lead_copy(t, q, j, to):
        columns = pl.ds(j * tile, tile)
        return mesh_copy(
            stack.at[:, :, columns], pivot.at[t, :, core, :, columns],
            lead_send.at[q, j], lead_recv.at[q, j], (a, to, c),
        )

    def leads(act):
        for q in range(1, trows):
            for j in range(trows):
                act(q, j)

    def send_lead(q, j):
        @pl.when(j >= r)
        def _():
            lead_copy(r, q, j, r ^ q).start()

    leads(send_lead)
    pivot[r, :, core] = stack[...]

    total = strip_part[pl.ds(pl.multiple_of(a // 2 * 2 * share, 2 * share), 2 * share)]
    for m, copy in enumerate(strips):
        copy.wait_recv()
        total = total + strip_in[m + 1]
    pair_sum[...] = total
    pair = mesh_copy(
        rows_of(pair_sum, 1 - parity), pair_in, pair_send, pair_recv, (a ^ 1, r, c)
    )
    pair.start()
    for copy in mine + theirs:
        copy.wait_recv()
    for copy in relays:
        copy.start()
    pair.wait_recv()
    total_ref[...] = rows_of(pair_sum, parity)[...] + pair_in[...]
    own_copy = pltpu.make_async_copy(total_ref, strip_out.at[a], own_sem)
    own_copy.start()
    wides = [
        mesh_copy(total_ref, strip_out.at[a], wide_send.at[m], wide_recv.at[m], (a ^ m, r, c))
        for m in [1] + [2 * m for m in beyond]
    ]
    for copy in wides:
        copy.start()
    wides[0].wait_recv()
    onward = [
        mesh_copy(
            strip_out.at[a ^ 1], strip_out.at[a ^ 1],
            relay_send.at[m], relay_recv.at[m], (a ^ (2 * m), r, c),
        )
        for m in beyond
    ]
    for copy in onward:
        copy.start()

    swaps = []
    for q in range(trows):
        t = r ^ q
        for j in range(trows if q else 0):
            @pl.when(j >= t)
            def _():
                lead_copy(t, q, j, t).wait_recv()

        copy = mesh_copy(
            pivot.at[t, :, core], pivot.at[t, :, core],
            core_send.at[q], core_recv.at[q], (a, r, c ^ 1),
        )
        copy.start()
        swaps.append(copy)

    def wait_lead(q, j):
        @pl.when(j >= r)
        def _():
            lead_copy(r, q, j, r ^ q).wait_send()

    leads(wait_lead)
    for copy in swaps + planes + relays + wides[1:] + onward:
        copy.wait()
    for copy in [keep_own, keep_mine, keep_theirs, own_copy] + keep_planes:
        copy.wait()
    sent = [swap, pair, wides[0]] + mine + theirs + stacked + strips
    for copy in sent:
        copy.wait_send()


def gather(own, piece, pivot_part, regs, arcs, trows, tcols):
    tile, width = pivot_part.shape
    rows, columns = own.shape
    share = tile // arcs
    depth = share // 2
    dma = pltpu.SemaphoreType.DMA
    vmem = pl.BlockSpec(memory_space=pltpu.VMEM)
    anywhere = pl.BlockSpec(memory_space=pl.ANY)
    return pl.pallas_call(
        gather_kernel,
        out_shape=(
            jax.ShapeDtypeStruct((trows, arcs, 2, depth, width), jnp.float32),
            jax.ShapeDtypeStruct((arcs, share, columns), jnp.float32),
            jax.ShapeDtypeStruct((2,) + own.shape, own.dtype),
            jax.ShapeDtypeStruct((tcols, 2) + piece.shape[1:], piece.dtype),
        ),
        in_specs=[vmem] * 4,
        out_specs=(vmem, anywhere, anywhere, anywhere),
        scratch_shapes=[
            pltpu.VMEM((arcs, share, width), jnp.float32),
            pltpu.VMEM((tile, columns), jnp.float32),
            pltpu.VMEM((arcs // 2, 2 * share, columns), jnp.float32),
            pltpu.VMEM((2, depth, width), jnp.float32),
            pltpu.VMEM((depth, width), jnp.float32),
            pltpu.VMEM((arcs, depth, width), jnp.float32),
            pltpu.VMEM((share, columns), jnp.float32),
            pltpu.VMEM(piece.shape[1:], piece.dtype),
            pltpu.VMEM(piece.shape, piece.dtype),
            pltpu.VMEM((2 * share, columns), jnp.float32),
            pltpu.VMEM((share, columns), jnp.float32),
            dma((tcols,)), dma,
            dma, dma,
            dma((tcols,)), dma((tcols,)),
            dma((tcols,)), dma((tcols,)),
            dma((trows, 2)), dma((trows, 2)),
            dma((arcs,)), dma((arcs,)),
            dma((tcols,)), dma,
            dma((arcs,)), dma((arcs,)),
            dma((trows, trows)), dma((trows, trows)),
            dma((trows,)), dma((trows,)),
            dma((arcs,)), dma((arcs,)),
            dma((arcs,)), dma((arcs,)),
            dma((arcs // 2,)), dma((arcs // 2,)),
            dma, dma,
            dma, dma((5,)),
        ],
        compiler_params=pltpu.CompilerParams(
            collective_id=0, has_side_effects=True, vmem_limit_bytes=40 * 1024 * 1024
        ),
        cost_estimate=pl.CostEstimate(
            flops=40 * 10**9, bytes_accessed=250_000_000, transcendentals=0
        ),
        name="gather",
    )(own, piece, pivot_part, regs)


def lead_kernel(
    pivot, plane, cross, both, diagonals, regs, high_ref, low_ref, strip_out, rows_out, normal,
    inverse_ref, tiles, received, diagonals_in,
    near_send, near_recv, far_send, far_recv, tile_send, tile_recv, own_sem,
    diagonal_send, diagonal_recv, row_send, row_recv, row_local,
):
    trows, arcs = strip_out.shape[:2]
    groups = cross.shape[0]
    a, r, c = lax.axis_index("arc"), lax.axis_index("trow"), lax.axis_index("tcol")
    up, down = lax.rem(r + 1, trows), lax.rem(r + trows - 1, trows)
    group = a // 2
    tcols = row_send.shape[1]
    tile = rows_out.shape[-1]
    greet(
        [(a ^ (2 * m), r, c) for m in range(1, groups)]
        + [(a, up, c), (a, down, c)]
        + [(a, r, c ^ q) for q in range(1, tcols)]
    )
    some = arcs // 2
    near = [
        mesh_copy(plane, strip_out.at[r], near_send.at[i], near_recv.at[i], (a, z, c))
        for i, z in enumerate((up, down))
    ]
    far = [
        mesh_copy(
            strip_out.at[z, part], strip_out.at[z, part],
            far_send.at[i], far_recv.at[i], (a, to, c),
        )
        for i, (z, part, to) in enumerate(
            ((down, pl.ds(0, some), up), (up, pl.ds(some, some), down))
        )
    ]
    exchanges = [
        mesh_copy(
            tiles.at[group ^ m], received.at[m - 1],
            tile_send.at[m - 1], tile_recv.at[m - 1], (a ^ (2 * m), r, c),
        )
        for m in range(1, groups)
    ]
    corners = [
        mesh_copy(
            diagonals.at[group ^ m], diagonals_in.at[m - 1],
            diagonal_send.at[m - 1], diagonal_recv.at[m - 1], (a ^ (2 * m), r, c),
        )
        for m in range(1, groups)
    ]

    holder = c == group
    spot = pl.ds(pl.multiple_of((lax.rem(a, 2) * trows + r) * tile, tile), tile)
    places = (r, up, down, lax.rem(r + 2, trows))

    def row_copies(i):
        source = (plane if i == 0 else strip_out.at[places[i]]).at[:, :, spot]
        target = rows_out.at[places[i]]
        away = [
            mesh_copy(source, target, row_send.at[i, q], row_recv.at[i], (a, r, c ^ q))
            for q in range(1, tcols)
        ]
        return away, pltpu.make_async_copy(source, target, row_local.at[i])

    def send_rows(i):
        @pl.when(holder)
        def _():
            away, here = row_copies(i)
            for copy in away:
                copy.start()
            here.start()

    for copy in near + corners:
        copy.start()
    send_rows(0)
    keep = pltpu.make_async_copy(plane, strip_out.at[r], own_sem)
    keep.start()

    def product(g):
        return lax.dot_general(
            cross[g], both[...], (((0,), (0,)), ((), ())), preferred_element_type=jnp.float32
        )

    eye = (
        lax.broadcasted_iota(jnp.int32, (tile, tile), 0)
        == lax.broadcasted_iota(jnp.int32, (tile, tile), 1)
    )

    def send_tile(i, _):
        g = group ^ (i + 1)
        tiles[g] = product(g).astype(tiles.dtype)

        @pl.when(c == g)
        def _():
            square = jnp.where(eye, 0.0, tiles[g, :, spot].astype(jnp.float32))
            tiles[g, :, spot] = square.astype(tiles.dtype)

        mesh_copy(
            tiles.at[g], received.at[i], tile_send.at[i], tile_recv.at[i], (a ^ (2 * (i + 1)), r, c)
        ).start()
        return 0

    lax.fori_loop(0, groups - 1, send_tile, 0)
    inverse_ref[...] = pivot[...].reshape(inverse_ref.shape)

    def before(k):
        @pl.when(k == 5)
        def _():
            for copy in near:
                copy.wait_recv()
            for copy in far:
                copy.start()
            send_rows(1)
            send_rows(2)

    eliminate(inverse_ref, before)
    for copy in far:
        copy.wait_recv()
    send_rows(3)

    def turn(i, _):
        here = pl.ds(pl.multiple_of(i * BLOCK, BLOCK), BLOCK)
        high_ref[:, here], low_ref[:, here] = halves(inverse_ref[here, :].T)
        return 0

    lax.fori_loop(0, inverse_ref.shape[0] // BLOCK, turn, 0)
    normal[...] = product(group)
    for copy in exchanges + corners:
        copy.wait()
    diagonal = regs[...]
    for i in range(groups - 1):
        normal[...] = normal[...] + received[i].astype(jnp.float32)
        diagonal = diagonal + diagonals_in[i]

    @pl.when(holder)
    def _():
        normal[:, spot] = normal[:, spot] + jnp.where(eye, diagonal, 0.0)

    @pl.when(holder)
    def _():
        for i in range(len(places)):
            away, here = row_copies(i)
            for copy in away:
                copy.wait_send()
            here.wait()

    @pl.when(jnp.logical_not(holder))
    def _():
        for i in range(len(places)):
            row_copies(i)[0][0].wait_recv()

    for copy in far:
        copy.wait_send()
    for copy in near:
        copy.wait_send()
    keep.wait()


def lead(pivot, plane, cross, both, diagonals, regs):
    trows, arcs = pivot.shape[:2]
    width = pivot.shape[-1]
    groups, _, tile = cross.shape
    columns = both.shape[1]
    half = both.dtype
    dma = pltpu.SemaphoreType.DMA
    vmem = pl.BlockSpec(memory_space=pltpu.VMEM)
    anywhere = pl.BlockSpec(memory_space=pl.ANY)
    return pl.pallas_call(
        lead_kernel,
        out_shape=(
            jax.ShapeDtypeStruct((width, width), half),
            jax.ShapeDtypeStruct((width, width), half),
            jax.ShapeDtypeStruct((trows,) + plane.shape, jnp.float32),
            jax.ShapeDtypeStruct((trows,) + plane.shape[:2] + (tile,), jnp.float32),
            jax.ShapeDtypeStruct((tile, columns), jnp.float32),
        ),
        in_specs=[vmem, anywhere, vmem, vmem, vmem, vmem],
        out_specs=(vmem, vmem, anywhere, anywhere, vmem),
        scratch_shapes=[
            pltpu.VMEM((width, width), jnp.float32),
            pltpu.VMEM((groups, tile, columns), half),
            pltpu.VMEM((groups - 1, tile, columns), half),
            pltpu.VMEM((groups - 1, 1, tile), jnp.float32),
            dma((2,)), dma((2,)),
            dma((2,)), dma((2,)),
            dma((groups - 1,)), dma((groups - 1,)),
            dma,
            dma((groups - 1,)), dma((groups - 1,)),
            dma((trows, groups)), dma((trows,)), dma((trows,)),
        ],
        compiler_params=pltpu.CompilerParams(
            collective_id=1, has_side_effects=True, vmem_limit_bytes=52 * 1024 * 1024
        ),
        cost_estimate=pl.CostEstimate(
            flops=80 * 10**9, bytes_accessed=250_000_000, transcendentals=0
        ),
        name="lead",
    )(pivot, plane, cross, both, diagonals, regs)


def halves(value):
    high = value.astype(jnp.bfloat16)
    return high, (value - high.astype(jnp.float32)).astype(jnp.bfloat16)


def products(left, right, dims):
    def one(x, y):
        return lax.dot_general(x, y, (dims, ((), ())), preferred_element_type=jnp.float32)

    return one(left[0], right[1]) + one(left[1], right[0]) + one(left[0], right[0])


def finish_kernel(
    first_ref, strip_ref, high_ref, low_ref, rows_ref, normal_ref, factor_out, normal_out,
    row_high, row_low,
):
    def factors(columns, first):
        high, low = halves(columns)
        ids = first + lax.broadcasted_iota(jnp.int32, (columns.shape[1], PANEL), 0)
        for p in range(PANELS):
            depth = (p + 1) * PANEL
            panel = slice(p * PANEL, depth)
            factor = products(
                (high[:depth], low[:depth]),
                (high_ref[:depth, panel], low_ref[:depth, panel]),
                ((0,), (0,)),
            )
            yield jnp.where(ids >= p * PANEL, factor, 0.0)

    @pl.when(pl.program_id(0) == 0)
    def _():
        for p, factor in enumerate(factors(rows_ref[...], first_ref[1])):
            row_high[p], row_low[p] = halves(factor)

    total = normal_ref[...]
    wide = strip_ref.shape[1]
    for p, factor in enumerate(factors(strip_ref[...], first_ref[0] + pl.program_id(0) * wide)):
        factor_out[p] = factor
        total = total - products((row_high[p], row_low[p]), halves(factor), ((1,), (1,)))
    normal_out[...] = total


def finish(strip, high, low, rows, normal, first):
    columns = strip.shape[1]
    tile = normal.shape[0]
    wide = 512
    return pl.pallas_call(
        finish_kernel,
        out_shape=(
            jax.ShapeDtypeStruct((PANELS, columns, PANEL), jnp.float32),
            jax.ShapeDtypeStruct(normal.shape, jnp.float32),
        ),
        grid=(columns // wide,),
        in_specs=[
            pl.BlockSpec(memory_space=pltpu.SMEM),
            pl.BlockSpec((LEAD, wide), lambda j: (0, j)),
            pl.BlockSpec((LEAD, LEAD), lambda j: (0, 0)),
            pl.BlockSpec((LEAD, LEAD), lambda j: (0, 0)),
            pl.BlockSpec((LEAD, tile), lambda j: (0, 0)),
            pl.BlockSpec((tile, wide), lambda j: (0, j)),
        ],
        out_specs=(
            pl.BlockSpec((PANELS, wide, PANEL), lambda j: (0, j, 0)),
            pl.BlockSpec((tile, wide), lambda j: (0, j)),
        ),
        scratch_shapes=[
            pltpu.VMEM((PANELS, tile, PANEL), jnp.bfloat16),
            pltpu.VMEM((PANELS, tile, PANEL), jnp.bfloat16),
        ],
        compiler_params=pltpu.CompilerParams(vmem_limit_bytes=52 * 1024 * 1024),
        cost_estimate=pl.CostEstimate(
            flops=14 * 10**9, bytes_accessed=25_000_000, transcendentals=0
        ),
        name="finish",
    )(first, strip, high, low, rows, normal)


def project(rows, basis, live):
    arcs, _, capacity = basis.shape
    blocks = rows.reshape(rows.shape[0], arcs, capacity, rows.shape[2])
    loadings = jnp.einsum(
        "alc,tacw->talw", basis, blocks, preferred_element_type=jnp.float32
    ).astype(jnp.bfloat16)
    cleaned = blocks.astype(jnp.float32) - jnp.einsum(
        "alc,talw->tacw", basis, loadings, preferred_element_type=jnp.float32
    )
    cleaned = jnp.where(live[None, :, :, None], cleaned, 0.0)
    return cleaned.astype(jnp.bfloat16).reshape(rows.shape)


def contract_rows(left_rows, right_rows):
    return lax.dot_general(
        left_rows, right_rows, (((0,), (0,)), ((), ())), preferred_element_type=jnp.float32
    )


def per_device(design, local_design, lengths, regularizer):
    row_count, col_width = design.shape
    tile = regularizer.shape[0]
    arc_total = lax.axis_size("arc")
    trow_total = lax.axis_size("trow")
    tcol_total = lax.axis_size("tcol")
    arc = lax.axis_index("arc")
    trow = lax.axis_index("trow")
    tcol = lax.axis_index("tcol")
    arcs_per_col = arc_total // tcol_total
    capacity = row_count // lengths.shape[0]

    live = jnp.arange(capacity, dtype=jnp.int32)[None, :] < lengths[:, None]

    basis = local_basis(local_design, lengths)
    own = project(design[None], basis, live)[0]
    piece = jnp.stack(
        [
            lax.dynamic_slice_in_dim(own, (e * trow_total + trow) * tile, tile, 1)
            for e in range(arcs_per_col)
        ]
    )

    row_ids = jnp.arange(tile, dtype=jnp.int32)
    lead_rows = trow * tile + row_ids
    lead_reg = jnp.where(arc == 0, regularizer, 0.0)

    lead_cols = jnp.arange(LEAD, dtype=jnp.int32)
    pivot_part = contract_rows(
        lax.dynamic_slice_in_dim(own, trow * tile, tile, 1), own[:, :LEAD]
    ) + jnp.where(lead_rows[:, None] == lead_cols[None, :], lead_reg[:, None], 0.0)

    lead_diagonal = jnp.where(
        (row_ids[:, None] == row_ids[None, :]) & (tcol == 0), lead_reg[:, None], 0.0
    )
    pivot, plane, both, cross = gather(
        own, piece, pivot_part, lead_diagonal, arc_total, trow_total, tcol_total
    )
    both = both.reshape(2 * row_count, col_width)
    cross = cross.reshape(tcol_total, 2 * row_count, tile)

    diagonals = jnp.sum(jnp.square(cross.astype(jnp.float32)), axis=1)[:, None, :]
    high, low, strip, row_strip, normal = lead(
        pivot, plane, cross, both, diagonals, regularizer[None, :]
    )
    first = jnp.stack([tcol * col_width, (arc * trow_total + trow) * tile])
    factors, normal = finish(
        strip.reshape(LEAD, col_width), high, low, row_strip.reshape(LEAD, tile), normal, first
    )
    return normal, factors


def solution(mesh):
    return jax.shard_map(
        per_device,
        mesh=mesh,
        in_specs=(P("arc", "tcol"), P("arc", None), P("arc"), P(("arc", "trow"))),
        out_specs=(P(("arc", "trow"), "tcol"), P(None, "tcol", None)),
        check_vma=False,
    )
```

```python
import jax
import jax.numpy as jnp
from jax import lax
from jax.experimental import pallas as pl
from jax.experimental.pallas import tpu as pltpu
from jax.sharding import PartitionSpec as P

PANEL = 512
PANELS = 2
LEAD = PANEL * PANELS
RIDGE = 0.1
BLOCK = 128
HIGHEST = lax.Precision.HIGHEST
AXES = ("arc", "trow", "tcol")


def spread(value):
    return jnp.broadcast_to(value, (8, 128))


def small_inverse(pivot):
    d = [list(row) for row in pivot]
    low = [[None] * 8 for _ in range(8)]
    root = [None] * 8
    for k in range(8):
        root[k] = lax.rsqrt(d[k][k])
        for i in range(k + 1, 8):
            low[i][k] = d[i][k] * root[k]
        for j in range(k + 1, 8):
            for i in range(j, 8):
                d[i][j] = d[i][j] - low[i][k] * low[j][k]
    inv = [[None] * 8 for _ in range(8)]
    for k in range(8):
        inv[k][k] = root[k]
        for i in range(k + 1, 8):
            acc = low[i][k] * inv[k][k]
            for m in range(k + 1, i):
                acc = acc + low[i][m] * inv[m][k]
            inv[i][k] = -acc * root[i]
    return inv


def inverse_factors(matrices):
    lane = lax.broadcasted_iota(jnp.int32, (8, 128), 1)
    sub = lax.broadcasted_iota(jnp.int32, (8, 128), 0)
    zero = jnp.zeros((8, 128), jnp.float32)
    work = [[m[8 * i : 8 * i + 8, :] for i in range(16)] for m in matrices]
    unit = [
        [jnp.where(lane == sub + 8 * i, 1.0, 0.0).astype(jnp.float32) for i in range(16)]
        for _ in matrices
    ]
    for t in range(16):
        for A, X in zip(work, unit):
            lead = 8 * t
            cols = [spread(A[t][:, lead + k : lead + k + 1]) for k in range(8)]
            pivot = [
                [spread(cols[k][i : i + 1, :]) if k <= i else None for k in range(8)]
                for i in range(8)
            ]
            inv = small_inverse(pivot)
            U, UX = zero, zero
            for k in range(8):
                c = zero
                for i in range(k, 8):
                    c = jnp.where(sub == i, inv[i][k], c)
                U = U + c * spread(A[t][k : k + 1, :])
                UX = UX + c * spread(X[t][k : k + 1, :])
            X[t] = UX
            if t == 15:
                continue
            V, VX = zero, zero
            for m in range(8):
                c = zero
                for k in range(m + 1):
                    c = jnp.where(sub == k, inv[m][k], c)
                V = V + c * spread(U[m : m + 1, :])
                VX = VX + c * spread(UX[m : m + 1, :])
            rows = [spread(V[k : k + 1, :]) for k in range(8)]
            rows_x = [spread(VX[k : k + 1, :]) for k in range(8)]
            for i in range(t + 1, 16):
                cs = [spread(A[i][:, lead + k : lead + k + 1]) for k in range(8)]
                for k in range(8):
                    A[i] = A[i] - cs[k] * rows[k]
                    X[i] = X[i] - cs[k] * rows_x[k]
    return [jnp.concatenate(X, 0) for X in unit]


def basis_kernel(lengths_ref, local_ref, basis_ref):
    arcs = basis_ref.shape[0]
    capacity = basis_ref.shape[2]
    row = lax.broadcasted_iota(jnp.int32, (capacity, BLOCK), 0)
    eye = (
        lax.broadcasted_iota(jnp.int32, (BLOCK, BLOCK), 0)
        == lax.broadcasted_iota(jnp.int32, (BLOCK, BLOCK), 1)
    )
    masked, normals = [], []
    for a in range(arcs):
        block = local_ref[a * capacity : (a + 1) * capacity, :].astype(jnp.float32)
        block = jnp.where(row < lengths_ref[a], block, 0.0)
        half = block.astype(jnp.bfloat16)
        normal = lax.dot_general(
            half, half, (((0,), (0,)), ((), ())), preferred_element_type=jnp.float32
        )
        masked.append(block)
        normals.append(normal + jnp.where(eye, RIDGE, 0.0))
    for a, inverse in enumerate(inverse_factors(normals)):
        basis = lax.dot_general(
            inverse,
            masked[a],
            (((1,), (1,)), ((), ())),
            precision=HIGHEST,
            preferred_element_type=jnp.float32,
        )
        basis_ref[a] = basis.astype(jnp.bfloat16)


def local_basis(local_design, lengths):
    arcs = lengths.shape[0]
    capacity = local_design.shape[0] // arcs
    return pl.pallas_call(
        basis_kernel,
        out_shape=jax.ShapeDtypeStruct((arcs, BLOCK, capacity), jnp.bfloat16),
        in_specs=[
            pl.BlockSpec(memory_space=pltpu.SMEM),
            pl.BlockSpec(memory_space=pltpu.VMEM),
        ],
        out_specs=pl.BlockSpec(memory_space=pltpu.VMEM),
        compiler_params=pltpu.CompilerParams(vmem_limit_bytes=32 * 1024 * 1024),
        cost_estimate=pl.CostEstimate(flops=10**9, bytes_accessed=30_000_000, transcendentals=0),
        name="local_basis",
    )(lengths, local_design)


def mesh_copy(src, dst, send, recv, device):
    return pltpu.make_async_remote_copy(
        src_ref=src,
        dst_ref=dst,
        send_sem=send,
        recv_sem=recv,
        device_id=device,
        device_id_type=pl.DeviceIdType.MESH,
    )


def greet(devices):
    barrier = pltpu.get_barrier_semaphore()
    for device in devices:
        pl.semaphore_signal(
            barrier, inc=1, device_id=device, device_id_type=pl.DeviceIdType.MESH
        )
    pl.semaphore_wait(barrier, len(devices))


def eliminate(out_ref, before):
    size = out_ref.shape[0]
    blocks = size // BLOCK
    col = lax.broadcasted_iota(jnp.int32, (BLOCK, size), 1)

    def step(k, _):
        before(k)
        base = pl.multiple_of(k * BLOCK, BLOCK)
        here = pl.ds(base, BLOCK)
        after = base + BLOCK
        inverse = inverse_factors([out_ref[here, here]])[0]
        out_ref[here, here] = jnp.where(
            lax.broadcasted_iota(jnp.int32, (BLOCK, BLOCK), 0)
            == lax.broadcasted_iota(jnp.int32, (BLOCK, BLOCK), 1),
            1.0,
            0.0,
        )
        lead_row = jnp.dot(
            inverse, out_ref[here, :], precision=HIGHEST, preferred_element_type=jnp.float32
        )
        coef = jnp.where(col >= after, lead_row, 0.0)

        def trail(first):
            below = slice(first, size)
            row = lax.broadcasted_iota(jnp.int32, (size - first, BLOCK), 0) + first
            out_ref[below, here] = jnp.where(row >= after, 0.0, out_ref[below, here])
            out_ref[below, :] = out_ref[below, :] - lax.dot_general(
                coef[:, below],
                lead_row,
                (((0,), (0,)), ((), ())),
                precision=HIGHEST,
                preferred_element_type=jnp.float32,
            )

        half = blocks // 2

        @pl.when(k < half)
        def _():
            trail(BLOCK)

        @pl.when((k >= half) & (k < blocks - 1))
        def _():
            trail((half + 1) * BLOCK)

        out_ref[here, :] = jnp.where(col < after, lead_row, 0.0)
        return 0

    lax.fori_loop(0, blocks, step, 0)


def gather_kernel(
    own, piece, pivot_part, regs, pivot, strip_out, both, cross,
    pivot_in, strip_part, strip_in, chunk, half, stack, total_ref, first, swap_in, pair_sum, pair_in,
    first_send, first_recv, swap_send, swap_recv, mine_send, mine_recv,
    theirs_send, theirs_recv, plane_send, plane_recv,
    part_send, part_recv, half_send, half_recv, stack_send, stack_recv,
    lead_send, lead_recv, core_send, core_recv, strip_send, strip_recv,
    wide_send, wide_recv, relay_send, relay_recv, pair_send, pair_recv, own_sem, local_sem,
):
    trows, arcs, cores, depth, width = pivot.shape
    share = total_ref.shape[0]
    tcols = half_send.shape[0]
    tile = width // trows
    a, r, c = lax.axis_index("arc"), lax.axis_index("trow"), lax.axis_index("tcol")
    core = lax.rem(c, 2)
    parity = lax.rem(a, 2)
    others = range(1, arcs)
    greet(
        [(a ^ m, r, c) for m in others]
        + [(a, r ^ q, c) for q in range(1, trows)]
        + [(a, r, c ^ q) for q in range(1, tcols)]
    )

    def rows_of(part, target):
        return part.at[pl.ds(pl.multiple_of(target * share, share), share)]

    parts = [
        mesh_copy(
            rows_of(pivot_part, a ^ m), pivot_in.at[m],
            part_send.at[m], part_recv.at[m], (a ^ m, r, c),
        )
        for m in others
    ]
    groups = arcs // 2
    beyond = range(1, groups)
    strips = [
        mesh_copy(
            strip_part.at[pl.ds(pl.multiple_of((a // 2 ^ m) * 2 * share, 2 * share), 2 * share)],
            strip_in.at[m],
            strip_send.at[m], strip_recv.at[m], (a ^ (2 * m), r, c),
        )
        for m in beyond
    ]
    firsts = [
        mesh_copy(piece.at[0], first, first_send.at[q], first_recv, (a, r, q))
        for q in (1, 2)
    ]
    first_on = mesh_copy(first, first, first_send.at[3], first_recv, (a, r, c ^ 1))
    swap = mesh_copy(piece, swap_in, swap_send, swap_recv, (a ^ 1, r, c))
    mine = [
        mesh_copy(
            piece.at[parity], cross.at[c, 0], mine_send.at[q], mine_recv.at[q], (a, r, c ^ q)
        )
        for q in (1, 2)
    ]
    theirs = [
        mesh_copy(
            swap_in.at[parity], cross.at[c, 1], theirs_send.at[q], theirs_recv.at[q], (a, r, c ^ q)
        )
        for q in (1, 2)
    ]
    relays = [
        mesh_copy(
            cross.at[c ^ 2], cross.at[c ^ 2], relay_send.at[0], relay_recv.at[0], (a, r, c ^ 1)
        )
    ]

    def spot(e):
        return pl.ds(pl.multiple_of((e * trows + r) * tile, tile), tile)

    planes = [
        mesh_copy(
            swap_in.at[e], both.at[1, :, spot(e)],
            plane_send.at[q, e], plane_recv.at[q, e], (a, r ^ q, c),
        )
        for q in range(1, trows)
        for e in range(piece.shape[0])
    ]

    @pl.when(c == 0)
    def _():
        for copy in firsts + parts:
            copy.start()
        first[...] = piece[0]
        for copy in firsts:
            copy.wait_send()

    @pl.when(c != 0)
    def _():
        first_on.wait_recv()

    @pl.when(c == 2)
    def _():
        first_on.start()

    swap.start()
    keep_mine = pltpu.make_async_copy(piece.at[parity], cross.at[c, 0], local_sem.at[0])
    keep_mine.start()
    keep_own = pltpu.make_async_copy(own, both.at[0], local_sem.at[4])
    keep_own.start()

    wide = 512
    for j in range(0, own.shape[1], wide):
        strip_part[:, j : j + wide] = lax.dot_general(
            first[...],
            own[:, j : j + wide],
            (((0,), (0,)), ((), ())),
            preferred_element_type=jnp.float32,
        )
    lead = pl.ds(pl.multiple_of(r * tile, tile), tile)
    strip_part[:, lead] = strip_part[:, lead] + regs[...]
    for copy in strips:
        copy.start()

    @pl.when(c == 0)
    def _():
        total = rows_of(pivot_part, a)[...]
        for m, copy in enumerate(parts):
            copy.wait_recv()
            total = total + pivot_in[m + 1]
        chunk[...] = total.reshape(chunk.shape)
        spreads = [
            mesh_copy(chunk.at[q % 2], half, half_send.at[q], half_recv, (a, r, q))
            for q in range(1, tcols)
        ]
        for copy in spreads:
            copy.start()
        half[...] = chunk[0]
        for copy in parts + spreads:
            copy.wait_send()

    @pl.when(c != 0)
    def _():
        mesh_copy(chunk.at[0], half, half_send.at[0], half_recv, (a, r, c ^ 1)).wait_recv()

    @pl.when(c == 2)
    def _():
        first_on.wait_send()

    stacked = [
        mesh_copy(half, stack.at[a], stack_send.at[m], stack_recv.at[m], (a ^ m, r, c))
        for m in others
    ]
    for copy in stacked:
        copy.start()
    stack[a] = half[...]
    swap.wait_recv()
    for copy in planes + mine + theirs:
        copy.start()
    keep_theirs = pltpu.make_async_copy(swap_in.at[parity], cross.at[c, 1], local_sem.at[1])
    keep_planes = [
        pltpu.make_async_copy(swap_in.at[e], both.at[1, :, spot(e)], local_sem.at[2 + e])
        for e in range(piece.shape[0])
    ]
    for copy in [keep_theirs] + keep_planes:
        copy.start()
    for copy in stacked:
        copy.wait_recv()

    def lead_copy(t, q, j, to):
        columns = pl.ds(j * tile, tile)
        return mesh_copy(
            stack.at[:, :, columns], pivot.at[t, :, core, :, columns],
            lead_send.at[q, j], lead_recv.at[q, j], (a, to, c),
        )

    def leads(act):
        for q in range(1, trows):
            for j in range(trows):
                act(q, j)

    def send_lead(q, j):
        @pl.when(j >= r)
        def _():
            lead_copy(r, q, j, r ^ q).start()

    leads(send_lead)
    pivot[r, :, core] = stack[...]

    total = strip_part[pl.ds(pl.multiple_of(a // 2 * 2 * share, 2 * share), 2 * share)]
    for m, copy in enumerate(strips):
        copy.wait_recv()
        total = total + strip_in[m + 1]
    pair_sum[...] = total
    pair = mesh_copy(
        rows_of(pair_sum, 1 - parity), pair_in, pair_send, pair_recv, (a ^ 1, r, c)
    )
    pair.start()
    for copy in mine + theirs:
        copy.wait_recv()
    for copy in relays:
        copy.start()
    pair.wait_recv()
    total_ref[...] = rows_of(pair_sum, parity)[...] + pair_in[...]
    own_copy = pltpu.make_async_copy(total_ref, strip_out.at[a], own_sem)
    own_copy.start()
    wides = [
        mesh_copy(total_ref, strip_out.at[a], wide_send.at[m], wide_recv.at[m], (a ^ m, r, c))
        for m in [1] + [2 * m for m in beyond]
    ]
    for copy in wides:
        copy.start()
    wides[0].wait_recv()
    onward = [
        mesh_copy(
            strip_out.at[a ^ 1], strip_out.at[a ^ 1],
            relay_send.at[m], relay_recv.at[m], (a ^ (2 * m), r, c),
        )
        for m in beyond
    ]
    for copy in onward:
        copy.start()

    swaps = []
    for q in range(trows):
        t = r ^ q
        for j in range(trows if q else 0):
            @pl.when(j >= t)
            def _():
                lead_copy(t, q, j, t).wait_recv()

        copy = mesh_copy(
            pivot.at[t, :, core], pivot.at[t, :, core],
            core_send.at[q], core_recv.at[q], (a, r, c ^ 1),
        )
        copy.start()
        swaps.append(copy)

    def wait_lead(q, j):
        @pl.when(j >= r)
        def _():
            lead_copy(r, q, j, r ^ q).wait_send()

    leads(wait_lead)
    for copy in swaps + planes + relays + wides[1:] + onward:
        copy.wait()
    for copy in [keep_own, keep_mine, keep_theirs, own_copy] + keep_planes:
        copy.wait()
    sent = [swap, pair, wides[0]] + mine + theirs + stacked + strips
    for copy in sent:
        copy.wait_send()


def gather(own, piece, pivot_part, regs, arcs, trows, tcols):
    tile, width = pivot_part.shape
    rows, columns = own.shape
    share = tile // arcs
    depth = share // 2
    dma = pltpu.SemaphoreType.DMA
    vmem = pl.BlockSpec(memory_space=pltpu.VMEM)
    anywhere = pl.BlockSpec(memory_space=pl.ANY)
    return pl.pallas_call(
        gather_kernel,
        out_shape=(
            jax.ShapeDtypeStruct((trows, arcs, 2, depth, width), jnp.float32),
            jax.ShapeDtypeStruct((arcs, share, columns), jnp.float32),
            jax.ShapeDtypeStruct((2,) + own.shape, own.dtype),
            jax.ShapeDtypeStruct((tcols, 2) + piece.shape[1:], piece.dtype),
        ),
        in_specs=[vmem] * 4,
        out_specs=(vmem, anywhere, anywhere, anywhere),
        scratch_shapes=[
            pltpu.VMEM((arcs, share, width), jnp.float32),
            pltpu.VMEM((tile, columns), jnp.float32),
            pltpu.VMEM((arcs // 2, 2 * share, columns), jnp.float32),
            pltpu.VMEM((2, depth, width), jnp.float32),
            pltpu.VMEM((depth, width), jnp.float32),
            pltpu.VMEM((arcs, depth, width), jnp.float32),
            pltpu.VMEM((share, columns), jnp.float32),
            pltpu.VMEM(piece.shape[1:], piece.dtype),
            pltpu.VMEM(piece.shape, piece.dtype),
            pltpu.VMEM((2 * share, columns), jnp.float32),
            pltpu.VMEM((share, columns), jnp.float32),
            dma((tcols,)), dma,
            dma, dma,
            dma((tcols,)), dma((tcols,)),
            dma((tcols,)), dma((tcols,)),
            dma((trows, 2)), dma((trows, 2)),
            dma((arcs,)), dma((arcs,)),
            dma((tcols,)), dma,
            dma((arcs,)), dma((arcs,)),
            dma((trows, trows)), dma((trows, trows)),
            dma((trows,)), dma((trows,)),
            dma((arcs,)), dma((arcs,)),
            dma((arcs,)), dma((arcs,)),
            dma((arcs // 2,)), dma((arcs // 2,)),
            dma, dma,
            dma, dma((5,)),
        ],
        compiler_params=pltpu.CompilerParams(
            collective_id=0, has_side_effects=True, vmem_limit_bytes=40 * 1024 * 1024
        ),
        cost_estimate=pl.CostEstimate(
            flops=40 * 10**9, bytes_accessed=250_000_000, transcendentals=0
        ),
        name="gather",
    )(own, piece, pivot_part, regs)


def lead_kernel(
    pivot, plane, cross, both, diagonals, regs, high_ref, low_ref, strip_out, rows_out, normal,
    inverse_ref, tiles, received, diagonals_in,
    near_send, near_recv, far_send, far_recv, tile_send, tile_recv, own_sem,
    diagonal_send, diagonal_recv, row_send, row_recv, row_local,
):
    trows, arcs = strip_out.shape[:2]
    groups = cross.shape[0]
    a, r, c = lax.axis_index("arc"), lax.axis_index("trow"), lax.axis_index("tcol")
    up, down = lax.rem(r + 1, trows), lax.rem(r + trows - 1, trows)
    group = a // 2
    tcols = row_send.shape[1]
    tile = rows_out.shape[-1]
    greet(
        [(a ^ (2 * m), r, c) for m in range(1, groups)]
        + [(a, up, c), (a, down, c)]
        + [(a, r, c ^ q) for q in range(1, tcols)]
    )
    some = arcs // 2
    near = [
        mesh_copy(plane, strip_out.at[r], near_send.at[i], near_recv.at[i], (a, z, c))
        for i, z in enumerate((up, down))
    ]
    far = [
        mesh_copy(
            strip_out.at[z, part], strip_out.at[z, part],
            far_send.at[i], far_recv.at[i], (a, to, c),
        )
        for i, (z, part, to) in enumerate(
            ((down, pl.ds(0, some), up), (up, pl.ds(some, some), down))
        )
    ]
    exchanges = [
        mesh_copy(
            tiles.at[group ^ m], received.at[m - 1],
            tile_send.at[m - 1], tile_recv.at[m - 1], (a ^ (2 * m), r, c),
        )
        for m in range(1, groups)
    ]
    corners = [
        mesh_copy(
            diagonals.at[group ^ m], diagonals_in.at[m - 1],
            diagonal_send.at[m - 1], diagonal_recv.at[m - 1], (a ^ (2 * m), r, c),
        )
        for m in range(1, groups)
    ]

    holder = c == group
    spot = pl.ds(pl.multiple_of((lax.rem(a, 2) * trows + r) * tile, tile), tile)
    places = (r, up, down, lax.rem(r + 2, trows))

    def row_copies(i):
        source = (plane if i == 0 else strip_out.at[places[i]]).at[:, :, spot]
        target = rows_out.at[places[i]]
        away = [
            mesh_copy(source, target, row_send.at[i, q], row_recv.at[i], (a, r, c ^ q))
            for q in range(1, tcols)
        ]
        return away, pltpu.make_async_copy(source, target, row_local.at[i])

    def send_rows(i):
        @pl.when(holder)
        def _():
            away, here = row_copies(i)
            for copy in away:
                copy.start()
            here.start()

    for copy in near + corners:
        copy.start()
    send_rows(0)
    keep = pltpu.make_async_copy(plane, strip_out.at[r], own_sem)
    keep.start()

    def product(g):
        return lax.dot_general(
            cross[g], both[...], (((0,), (0,)), ((), ())), preferred_element_type=jnp.float32
        )

    eye = (
        lax.broadcasted_iota(jnp.int32, (tile, tile), 0)
        == lax.broadcasted_iota(jnp.int32, (tile, tile), 1)
    )

    def send_tile(i, _):
        g = group ^ (i + 1)
        tiles[g] = product(g).astype(tiles.dtype)

        @pl.when(c == g)
        def _():
            square = jnp.where(eye, 0.0, tiles[g, :, spot].astype(jnp.float32))
            tiles[g, :, spot] = square.astype(tiles.dtype)

        mesh_copy(
            tiles.at[g], received.at[i], tile_send.at[i], tile_recv.at[i], (a ^ (2 * (i + 1)), r, c)
        ).start()
        return 0

    lax.fori_loop(0, groups - 1, send_tile, 0)
    inverse_ref[...] = pivot[...].reshape(inverse_ref.shape)

    def before(k):
        @pl.when(k == 5)
        def _():
            for copy in near:
                copy.wait_recv()
            for copy in far:
                copy.start()
            send_rows(1)
            send_rows(2)

    eliminate(inverse_ref, before)

    def turn(i, _):
        here = pl.ds(pl.multiple_of(i * BLOCK, BLOCK), BLOCK)
        high_ref[:, here], low_ref[:, here] = halves(inverse_ref[here, :].T)
        return 0

    lax.fori_loop(0, inverse_ref.shape[0] // BLOCK, turn, 0)
    for copy in far:
        copy.wait_recv()
    send_rows(3)
    normal[...] = product(group)
    for copy in exchanges + corners:
        copy.wait()
    diagonal = regs[...]
    for i in range(groups - 1):
        normal[...] = normal[...] + received[i].astype(jnp.float32)
        diagonal = diagonal + diagonals_in[i]

    @pl.when(holder)
    def _():
        normal[:, spot] = normal[:, spot] + jnp.where(eye, diagonal, 0.0)

    @pl.when(holder)
    def _():
        for i in range(len(places)):
            away, here = row_copies(i)
            for copy in away:
                copy.wait_send()
            here.wait()

    @pl.when(jnp.logical_not(holder))
    def _():
        for i in range(len(places)):
            row_copies(i)[0][0].wait_recv()

    for copy in far:
        copy.wait_send()
    for copy in near:
        copy.wait_send()
    keep.wait()


def lead(pivot, plane, cross, both, diagonals, regs):
    trows, arcs = pivot.shape[:2]
    width = pivot.shape[-1]
    groups, _, tile = cross.shape
    columns = both.shape[1]
    half = both.dtype
    dma = pltpu.SemaphoreType.DMA
    vmem = pl.BlockSpec(memory_space=pltpu.VMEM)
    anywhere = pl.BlockSpec(memory_space=pl.ANY)
    return pl.pallas_call(
        lead_kernel,
        out_shape=(
            jax.ShapeDtypeStruct((width, width), half),
            jax.ShapeDtypeStruct((width, width), half),
            jax.ShapeDtypeStruct((trows,) + plane.shape, jnp.float32),
            jax.ShapeDtypeStruct((trows,) + plane.shape[:2] + (tile,), jnp.float32),
            jax.ShapeDtypeStruct((tile, columns), jnp.float32),
        ),
        in_specs=[vmem, anywhere, vmem, vmem, vmem, vmem],
        out_specs=(vmem, vmem, anywhere, anywhere, vmem),
        scratch_shapes=[
            pltpu.VMEM((width, width), jnp.float32),
            pltpu.VMEM((groups, tile, columns), half),
            pltpu.VMEM((groups - 1, tile, columns), half),
            pltpu.VMEM((groups - 1, 1, tile), jnp.float32),
            dma((2,)), dma((2,)),
            dma((2,)), dma((2,)),
            dma((groups - 1,)), dma((groups - 1,)),
            dma,
            dma((groups - 1,)), dma((groups - 1,)),
            dma((trows, groups)), dma((trows,)), dma((trows,)),
        ],
        compiler_params=pltpu.CompilerParams(
            collective_id=1, has_side_effects=True, vmem_limit_bytes=52 * 1024 * 1024
        ),
        cost_estimate=pl.CostEstimate(
            flops=80 * 10**9, bytes_accessed=250_000_000, transcendentals=0
        ),
        name="lead",
    )(pivot, plane, cross, both, diagonals, regs)


def halves(value):
    high = value.astype(jnp.bfloat16)
    return high, (value - high.astype(jnp.float32)).astype(jnp.bfloat16)


def products(left, right, dims):
    def one(x, y):
        return lax.dot_general(x, y, (dims, ((), ())), preferred_element_type=jnp.float32)

    return one(left[0], right[1]) + one(left[1], right[0]) + one(left[0], right[0])


def finish_kernel(
    first_ref, strip_ref, high_ref, low_ref, rows_ref, normal_ref, factor_out, normal_out,
    row_high, row_low,
):
    def factors(columns, first):
        high, low = halves(columns)
        ids = first + lax.broadcasted_iota(jnp.int32, (columns.shape[1], PANEL), 0)
        for p in range(PANELS):
            depth = (p + 1) * PANEL
            panel = slice(p * PANEL, depth)
            factor = products(
                (high[:depth], low[:depth]),
                (high_ref[:depth, panel], low_ref[:depth, panel]),
                ((0,), (0,)),
            )
            yield jnp.where(ids >= p * PANEL, factor, 0.0)

    @pl.when(pl.program_id(0) == 0)
    def _():
        for p, factor in enumerate(factors(rows_ref[...], first_ref[1])):
            row_high[p], row_low[p] = halves(factor)

    total = normal_ref[...]
    wide = strip_ref.shape[1]
    for p, factor in enumerate(factors(strip_ref[...], first_ref[0] + pl.program_id(0) * wide)):
        factor_out[p] = factor
        total = total - products((row_high[p], row_low[p]), halves(factor), ((1,), (1,)))
    normal_out[...] = total


def finish(strip, high, low, rows, normal, first):
    columns = strip.shape[1]
    tile = normal.shape[0]
    wide = 1024
    return pl.pallas_call(
        finish_kernel,
        out_shape=(
            jax.ShapeDtypeStruct((PANELS, columns, PANEL), jnp.float32),
            jax.ShapeDtypeStruct(normal.shape, jnp.float32),
        ),
        grid=(columns // wide,),
        in_specs=[
            pl.BlockSpec(memory_space=pltpu.SMEM),
            pl.BlockSpec((LEAD, wide), lambda j: (0, j)),
            pl.BlockSpec((LEAD, LEAD), lambda j: (0, 0)),
            pl.BlockSpec((LEAD, LEAD), lambda j: (0, 0)),
            pl.BlockSpec((LEAD, tile), lambda j: (0, 0)),
            pl.BlockSpec((tile, wide), lambda j: (0, j)),
        ],
        out_specs=(
            pl.BlockSpec((PANELS, wide, PANEL), lambda j: (0, j, 0)),
            pl.BlockSpec((tile, wide), lambda j: (0, j)),
        ),
        scratch_shapes=[
            pltpu.VMEM((PANELS, tile, PANEL), jnp.bfloat16),
            pltpu.VMEM((PANELS, tile, PANEL), jnp.bfloat16),
        ],
        compiler_params=pltpu.CompilerParams(vmem_limit_bytes=52 * 1024 * 1024),
        cost_estimate=pl.CostEstimate(
            flops=14 * 10**9, bytes_accessed=25_000_000, transcendentals=0
        ),
        name="finish",
    )(first, strip, high, low, rows, normal)


def project(rows, basis, live):
    arcs, _, capacity = basis.shape
    blocks = rows.reshape(rows.shape[0], arcs, capacity, rows.shape[2])
    loadings = jnp.einsum(
        "alc,tacw->talw", basis, blocks, preferred_element_type=jnp.float32
    ).astype(jnp.bfloat16)
    cleaned = blocks.astype(jnp.float32) - jnp.einsum(
        "alc,talw->tacw", basis, loadings, preferred_element_type=jnp.float32
    )
    cleaned = jnp.where(live[None, :, :, None], cleaned, 0.0)
    return cleaned.astype(jnp.bfloat16).reshape(rows.shape)


def contract_rows(left_rows, right_rows):
    return lax.dot_general(
        left_rows, right_rows, (((0,), (0,)), ((), ())), preferred_element_type=jnp.float32
    )


def per_device(design, local_design, lengths, regularizer):
    row_count, col_width = design.shape
    tile = regularizer.shape[0]
    arc_total = lax.axis_size("arc")
    trow_total = lax.axis_size("trow")
    tcol_total = lax.axis_size("tcol")
    arc = lax.axis_index("arc")
    trow = lax.axis_index("trow")
    tcol = lax.axis_index("tcol")
    arcs_per_col = arc_total // tcol_total
    capacity = row_count // lengths.shape[0]

    live = jnp.arange(capacity, dtype=jnp.int32)[None, :] < lengths[:, None]

    basis = local_basis(local_design, lengths)
    own = project(design[None], basis, live)[0]
    piece = jnp.stack(
        [
            lax.dynamic_slice_in_dim(own, (e * trow_total + trow) * tile, tile, 1)
            for e in range(arcs_per_col)
        ]
    )

    row_ids = jnp.arange(tile, dtype=jnp.int32)
    lead_rows = trow * tile + row_ids
    lead_reg = jnp.where(arc == 0, regularizer, 0.0)

    lead_cols = jnp.arange(LEAD, dtype=jnp.int32)
    pivot_part = contract_rows(
        lax.dynamic_slice_in_dim(own, trow * tile, tile, 1), own[:, :LEAD]
    ) + jnp.where(lead_rows[:, None] == lead_cols[None, :], lead_reg[:, None], 0.0)

    lead_diagonal = jnp.where(
        (row_ids[:, None] == row_ids[None, :]) & (tcol == 0), lead_reg[:, None], 0.0
    )
    pivot, plane, both, cross = gather(
        own, piece, pivot_part, lead_diagonal, arc_total, trow_total, tcol_total
    )
    both = both.reshape(2 * row_count, col_width)
    cross = cross.reshape(tcol_total, 2 * row_count, tile)

    diagonals = jnp.sum(jnp.square(cross.astype(jnp.float32)), axis=1)[:, None, :]
    high, low, strip, row_strip, normal = lead(
        pivot, plane, cross, both, diagonals, regularizer[None, :]
    )
    first = jnp.stack([tcol * col_width, (arc * trow_total + trow) * tile])
    factors, normal = finish(
        strip.reshape(LEAD, col_width), high, low, row_strip.reshape(LEAD, tile), normal, first
    )
    return normal, factors


def solution(mesh):
    return jax.shard_map(
        per_device,
        mesh=mesh,
        in_specs=(P("arc", "tcol"), P("arc", None), P("arc"), P(("arc", "trow"))),
        out_specs=(P(("arc", "trow"), "tcol"), P(None, "tcol", None)),
        check_vma=False,
    )
```
